256 devices in a mesh: ctx: 16 (over y_hi, x, core), mp: 16 (over y_lo, z).
Axes of the slice: x: 4, y: 4 (y_hi: 2, y_lo: 2; y = y_hi * 2 + y_lo), z: 8, core: 2. Of those that a mesh axis runs over, the one named last changes fastest.
Arguments:
- token_ids: int32 [12288], P('ctx'), may hold values from 0 to 511
- feature_table: bfloat16 [512, 3, 4096], P(None, None, 'mp'), may hold values from -6 to 6
- short_filter: float32 [3, 3, 4096], P(None, None, 'mp'), may hold values from -4 to 4
- rates: float32 [4096, 16], P('mp'), may hold values from 1 to 384
- residues: float32 [4096, 16], P('mp'), may hold values from -1.5 to 1.5
- skip_weight: float32 [4096], P('mp'), may hold values from -4 to 4
- w_qkv: bfloat16 [4096, 3, 4096], P(None, None, 'mp'), may hold values from -2 to 2
Outputs:
- hyena_out: bfloat16 [12288, 4096], P('ctx', 'mp')
- attended: bfloat16 [12288, 4096], P('ctx', 'mp')
The draws below stay inside these ranges and needn't reach their ends.
All inputs are finite; a program needn't handle non-finite values.
Results may differ from the reference program's by a relative error of at most 0.039.
The reference program's roundings to bfloat16 on the way count: a program that leaves them out, or rounds other values in their place, can miss the bound.
Values may be sent and summed in bfloat16 or wider, within the bound.
A program may use at most 128 MiB of HBM per device.

```python
import math
import jax
import jax.numpy as jnp
import numpy as np
from jax import lax

HC = 4096
HEADS = 32
HEAD_DIM = 128
MODES = 16
TAPS = 3
VOCAB = 512
TOKENS = 12288


def draw_rates(key, part):
    key = jax.random.fold_in(key, 11)
    first_key = jax.random.fold_in(key, 0)
    array_shape = (HC, MODES)
    upper = math.log(TOKENS // 32)
    return jnp.exp(jax.random.uniform(first_key, array_shape, jnp.float32, 0.0, upper))


def draw_w_qkv(key, part):
    key = jax.random.fold_in(key, 23)
    array_shape = (HC, 3, HEADS * HEAD_DIM)
    raw_values = jax.random.normal(key, array_shape, jnp.float32)
    return (raw_values / math.sqrt(HC)).astype(jnp.bfloat16)


def place_ends(result, key, smallest, largest):
    index_at = [jax.random.randint(jax.random.fold_in(key, axis), (), 0, length) for axis, length in enumerate(result.shape)]
    longest = result.shape.index(max(result.shape))
    next_to = index_at[:longest] + [(index_at[longest] + 1) % result.shape[longest]] + index_at[longest + 1:]
    return result.at[tuple(index_at)].set(smallest).at[tuple(next_to)].set(largest)


def steps_of(rng, extent, pieces, least, high):
    def one(dim, parts):
        heights = jax.random.uniform(jax.random.fold_in(jax.random.fold_in(rng, 6), dim), (parts,), jnp.float32, least / len(pieces), high / len(pieces))
        return jnp.repeat(jnp.exp(heights), extent[dim] // parts).reshape((-1,) + (1,) * (len(extent) - dim - 1))

    loudness = one(*pieces[0])
    for cut in pieces[1:]:
        loudness = loudness * one(*cut)
    return loudness


def rank_bounds(number_of, slope):
    weights = [(1 << 20) // math.isqrt(rank ** slope) + 1 for rank in range(1, number_of + 1)]
    scale = 1 + sum(weights) // (1 << 30)
    return np.cumsum(np.array([max(1, weight // scale) for weight in weights]))


def ranked_ids(own_key, dims, amount, lean):
    listing = rank_bounds(amount, lean)
    ticket = jax.random.randint(jax.random.fold_in(own_key, 1), dims, 0, int(listing[amount - 1]))
    rank = jnp.searchsorted(jnp.asarray(listing, jnp.int32), ticket, side="right")
    return jax.random.permutation(jax.random.fold_in(own_key, 2), amount)[rank].astype(jnp.int32)


def scatter_about(stream_key, extent, spread, most, shards=(), held_as=jnp.bfloat16):
    values = spread * jax.random.normal(stream_key, extent, jnp.float32)
    if shards:
        values = values * steps_of(stream_key, extent, shards, -0.22, 0.18)
    return jnp.clip(values, -most, most).astype(held_as)


def setup_inputs(seed: int = 0) -> dict:
    streams_of = jax.random.split(jax.random.key(seed), 8)
    return {
        "token_ids": place_ends(ranked_ids(streams_of[0], (TOKENS,), VOCAB, 1), jax.random.fold_in(streams_of[0], 3), 0, VOCAB - 1).astype(jnp.int32),
        "feature_table": scatter_about(streams_of[1], (VOCAB, 3, HC), 1.0, 6.0, ((2, 16),)),
        "short_filter": scatter_about(streams_of[2], (TAPS, 3, HC), 0.6, 4.0, ((2, 16),), jnp.float32),
        "rates": draw_rates(jax.random.fold_in(streams_of[7], 71), 0),
        "residues": scatter_about(streams_of[4], (HC, MODES), MODES ** -0.5, 1.5, ((0, 16),), jnp.float32),
        "skip_weight": scatter_about(streams_of[5], (HC,), 1.0, 4.0, ((0, 16),), jnp.float32),
        "w_qkv": draw_w_qkv(jax.random.fold_in(streams_of[7], 71), 0),
    }


NEG_FILL = -1e+30
NORM_EPSILON = 1e-06

def reference(token_ids, feature_table, short_filter, rates, residues, skip_weight, w_qkv):
    total_len = token_ids.shape[0]
    one_hot = (token_ids[:, None] == jnp.arange(VOCAB, dtype=jnp.int32)[None, :]).astype(jnp.bfloat16)
    features = jnp.dot(one_hot, feature_table.reshape(VOCAB, -1), preferred_element_type=jnp.float32)
    features = features.reshape(total_len, 3, HC)
    padded = jnp.concatenate([jnp.zeros((TAPS - 1, 3, HC), jnp.float32), features], axis=0)
    smoothed = short_filter[0][None] * padded[TAPS - 1:TAPS - 1 + total_len]
    for tap_index in range(1, TAPS):
        smoothed = smoothed + short_filter[tap_index][None] * padded[TAPS - 1 - tap_index:TAPS - 1 - tap_index + total_len]
    gate_prod = smoothed[:, 1] * smoothed[:, 2]
    damping = rates / TOKENS
    mode_weight = residues * jnp.sqrt(-jnp.expm1(-2.0 * damping))
    decay = jnp.exp(-damping)

    def advance(carried, gate_row):
        updated = decay * carried + gate_row[:, None]
        return (updated, lax.optimization_barrier(jnp.sum(mode_weight * updated, axis=1)))
    _, convolved = lax.scan(advance, jnp.zeros((HC, MODES), jnp.float32), gate_prod)
    hyena_out = (smoothed[:, 0] * (convolved + skip_weight[None, :] * gate_prod)).astype(jnp.bfloat16)
    projected = jnp.dot(hyena_out, w_qkv.reshape(HC, -1), preferred_element_type=jnp.float32)
    projected = projected.reshape(total_len, 3, HEADS * HEAD_DIM)
    wide = hyena_out.astype(jnp.float32)
    squares = lax.optimization_barrier(jnp.sum(wide * wide, axis=1))
    projected = projected * lax.rsqrt(squares / HC + NORM_EPSILON)[:, None, None]
    queries = projected[:, 0].astype(jnp.bfloat16).reshape(total_len, HEADS, HEAD_DIM)
    key_rows = projected[:, 1].astype(jnp.bfloat16).reshape(total_len, HEADS, HEAD_DIM)
    value_rows = projected[:, 2].astype(jnp.bfloat16).reshape(total_len, HEADS, HEAD_DIM)
    queries = jnp.transpose(queries, (1, 0, 2))
    key_rows = jnp.transpose(key_rows, (1, 0, 2))
    value_rows = jnp.transpose(value_rows, (1, 0, 2))
    block_len = math.gcd(total_len, 512)
    block_count = total_len // block_len
    scale = 1.0 / math.sqrt(HEAD_DIM)
    key_pos = jnp.arange(total_len, dtype=jnp.int32)

    def head_attention(head_parts):
        head_queries, head_keys, head_values = head_parts

        def block_rows(number):
            block = lax.dynamic_slice_in_dim(head_queries, number * block_len, block_len, 0)
            query_pos = number * block_len + jnp.arange(block_len, dtype=jnp.int32)
            scores = jnp.dot(block, head_keys.T, preferred_element_type=jnp.float32) * scale
            allowed = key_pos[None, :] <= query_pos[:, None]
            scores = jnp.where(allowed, scores, NEG_FILL)
            highest = lax.optimization_barrier(jnp.max(scores, axis=1, keepdims=True))
            weights = jnp.where(allowed, jnp.exp(scores - highest), 0.0)
            totals = lax.optimization_barrier(jnp.sum(weights, axis=1))
            summed = jnp.dot(weights.astype(jnp.bfloat16), head_values, preferred_element_type=jnp.float32)
            return summed / totals[:, None]
        blocks = lax.map(block_rows, jnp.arange(block_count, dtype=jnp.int32))
        return blocks.reshape(total_len, HEAD_DIM)
    per_head = lax.map(head_attention, (queries, key_rows, value_rows))
    attended = jnp.transpose(per_head, (1, 0, 2)).reshape(total_len, HEADS * HEAD_DIM).astype(jnp.bfloat16)
    return (hyena_out, attended)
```

```python
import functools
import math

import jax
import jax.numpy as jnp
from jax import lax
from jax.experimental import pallas as pl
from jax.experimental.pallas import tpu as pltpu
from jax.sharding import PartitionSpec as P

MESH = pl.DeviceIdType.MESH
HEAD_DIM = 128
TAPS = 3
SEGS = 8
NEG_FILL = -1e30
NORM_EPSILON = 1e-06

CTX = 16
MP = 16
PLANE = 8
CHUNKS = 4
Q_TILE = 256


def mixer_kernel(
    ids_ref, table_hbm, filt_ref, rates_ref, resid_ref, skip_ref, w_hbm,
    hyena_hbm, att_hbm,
    table, w, feats, gate, lead, rim, decay, weight, ends, starts, states,
    x, kv, qs, kv_out, q_out, q_acc, q_max, att,
    local_sem, rim_sem, state_send, state_recv,
    y_send, y_recv, z_send, z_recv,
    h_send, h_recv, c_send, c_recv, r_send, r_recv, o_sem,
):
    rows = feats.shape[1] - 8
    chans = feats.shape[2]
    modes = decay.shape[0]
    steps = rows // SEGS
    part = rows // CHUNKS
    half = part // 2
    all_chans = x.shape[1]
    total_len = CTX * rows

    me = lax.axis_index("ctx")
    mp = lax.axis_index("mp")
    core = me % 2
    xpos = (me // 2) % 4
    yhi = me // 8
    zpos = mp % PLANE
    ylo = mp // PLANE
    sibling = me + 1 - 2 * core
    opposite = (me + 8) % CTX
    x_right = yhi * 8 + 2 * ((xpos + 1) % 4) + core
    x_left = yhi * 8 + 2 * ((xpos + 3) % 4) + core
    x_far = yhi * 8 + 2 * ((xpos + 2) % 4) + core
    z_right = ylo * PLANE + (zpos + 1) % PLANE
    z_left = ylo * PLANE + (zpos + PLANE - 1) % PLANE
    y_other = (1 - ylo) * PLANE + zpos

    def to_ctx(src, dst, send, recv, target):
        return pltpu.make_async_remote_copy(
            src_ref=src, dst_ref=dst, send_sem=send, recv_sem=recv,
            device_id={"ctx": target}, device_id_type=MESH,
        )

    def to_mp(src, dst, send, recv, target):
        return pltpu.make_async_remote_copy(
            src_ref=src, dst_ref=dst, send_sem=send, recv_sem=recv,
            device_id={"mp": target}, device_id_type=MESH,
        )

    table_copy = pltpu.make_async_copy(table_hbm, table, local_sem.at[0])
    table_copy.start()
    w_copy = pltpu.make_async_copy(w_hbm, w, local_sem.at[1])
    w_copy.start()

    barrier = pltpu.get_barrier_semaphore()
    for k in range(1, CTX):
        pl.semaphore_signal(
            barrier, inc=1, device_id={"ctx": (me + k) % CTX}, device_id_type=MESH
        )
    for other in (z_right, z_left, y_other):
        pl.semaphore_signal(barrier, inc=1, device_id={"mp": other}, device_id_type=MESH)
    pl.semaphore_wait(barrier, CTX - 1 + 3)

    rim_copy = to_ctx(
        ids_ref.at[:, pl.ds(rows - 128, 128)], rim, rim_sem.at[0], rim_sem.at[1], (me + 1) % CTX
    )
    rim_copy.start()

    vocab = table.shape[1]

    def looked(ids, feature):
        at = lax.broadcasted_iota(jnp.int32, (vocab, ids.shape[1]), 0)
        hot = (at == ids).astype(jnp.float32).astype(jnp.bfloat16)
        return lax.dot_general(
            hot, table[feature], (((0,), (0,)), ((), ())), preferred_element_type=jnp.float32
        )

    damping = rates_ref[...] / total_len
    twice = 2.0 * damping
    small = twice * (
        1.0
        - twice
        * (
            0.5
            - twice
            * (1.0 / 6 - twice * (1.0 / 24 - twice * (1.0 / 120 - twice * (1.0 / 720))))
        )
    )
    grown = jnp.where(twice < 0.1, small, 1.0 - jnp.exp(-twice))
    mode_weight = resid_ref[...] * jnp.sqrt(grown)
    one_step = jnp.exp(-damping)
    for r in range(modes):
        decay[r] = jnp.broadcast_to(one_step[r : r + 1, :], (SEGS, chans))
        weight[r] = jnp.broadcast_to(mode_weight[r : r + 1, :], (SEGS, chans))

    table_copy.wait()
    for j in range(3):
        feats[j, 8:, :] = looked(ids_ref[...], j)
    rim_copy.wait_recv()
    for j in range(3):
        before = looked(rim[...], j)[120:128, :]
        feats[j, 0:8, :] = jnp.where(me > 0, before, 0.0)

    def smooth(j, at, count):
        total = filt_ref[0, j : j + 1, :] * feats[j, 8 + at : 8 + at + count, :]
        for tap in range(1, TAPS):
            total = total + filt_ref[tap, j : j + 1, :] * feats[
                j, 8 + at - tap : 8 + at - tap + count, :
            ]
        return total

    groups = [(g, slice(g * 128, (g + 1) * 128)) for g in range(chans // 128)]
    for at in range(0, rows, 96):
        gated = smooth(1, at, 96) * smooth(2, at, 96)
        led = smooth(0, at, 96)
        for g, lanes in groups:
            gate[g, at : at + 96, :] = gated[:, lanes]
            lead[g, at : at + 96, :] = led[:, lanes]

    for g, lanes in groups:
        fade = decay[:, :, lanes]

        def ended(i, state, g=g, fade=fade):
            row = gate[g, pl.ds(i, SEGS, stride=steps), :]
            return fade * state + row[None]

        ends[:, :, lanes] = lax.fori_loop(
            0, steps, ended, jnp.zeros((modes, SEGS, 128), jnp.float32)
        )
    segment_fade = jnp.exp(-damping * steps)
    running = jnp.zeros((modes, chans), jnp.float32)
    for j in range(SEGS):
        starts[:, j, :] = running
        running = segment_fade * running + ends[:, j, :]
    states[me] = running
    state_copies = []
    for k in range(1, CTX):
        copy = to_ctx(
            states.at[me], states.at[me], state_send.at[k - 1], state_recv.at[k - 1],
            (me + k) % CTX,
        )
        copy.start()
        state_copies.append(copy)
    for k in range(1, CTX):
        source = (me + CTX - k) % CTX
        to_ctx(
            states.at[source], states.at[source], state_send.at[k - 1], state_recv.at[k - 1],
            (me + k) % CTX,
        ).wait_recv()

    def gathered(k, total):
        gap = jnp.maximum(me - 1 - k, 0).astype(jnp.float32) * rows
        return total + jnp.where(k < me, jnp.exp(-damping * gap) * states[k], 0.0)

    incoming = lax.fori_loop(0, CTX, gathered, jnp.zeros((modes, chans), jnp.float32))
    for j in range(SEGS):
        starts[:, j, :] += jnp.exp(-damping * (steps * j)) * incoming

    for g, lanes in groups:
        fade = decay[:, :, lanes]
        skip = skip_ref[:, lanes]

        def stepped(i, state, g=g, lanes=lanes, fade=fade, skip=skip):
            at = pl.ds(i, SEGS, stride=steps)
            row = gate[g, at, :]
            state = fade * state + row[None]
            conv = jnp.sum(weight[:, :, lanes] * state, axis=0)
            gate[g, at, :] = lead[g, at, :] * (conv + skip * row)
            return state

        lax.fori_loop(0, steps, stepped, starts[:, :, lanes])

    def columns(ylo_at, z_at):
        return pl.ds(pl.multiple_of((ylo_at * PLANE + z_at) * chans, chans), chans)

    mine = columns(ylo, zpos)
    x[:, mine] = jnp.concatenate([gate[g] for g, _ in groups], axis=1).astype(jnp.bfloat16)
    hyena_copy = pltpu.make_async_copy(x.at[:, mine], hyena_hbm, local_sem.at[2])
    hyena_copy.start()

    def z_copy(n, plane, step, direction):
        away = step - 1
        origin = (zpos + PLANE - away) % PLANE if direction == 0 else (zpos + away) % PLANE
        target = z_right if direction == 0 else z_left
        count, shift = (half, direction * half) if step == 4 else (part, 0)
        at = pl.ds(pl.multiple_of(n * part + shift, 16), count)
        ref = x.at[at, columns(ylo if plane == 0 else 1 - ylo, origin)]
        k = ((n * 2 + plane) * 4 + step - 1) * 2 + direction
        return to_mp(ref, ref, z_send.at[k], z_recv.at[k], target)

    def z_wait(n, plane, step, direction):
        origin = (zpos + PLANE - step) % PLANE if direction == 0 else (zpos + step) % PLANE
        target = z_right if direction == 0 else z_left
        count, shift = (half, direction * half) if step == 4 else (part, 0)
        at = pl.ds(pl.multiple_of(n * part + shift, 16), count)
        ref = x.at[at, columns(ylo if plane == 0 else 1 - ylo, origin)]
        k = ((n * 2 + plane) * 4 + step - 1) * 2 + direction
        to_mp(ref, ref, z_send.at[k], z_recv.at[k], target).wait_recv()

    def y_copy(n, ylo_at):
        ref = x.at[pl.ds(pl.multiple_of(n * part, 16), part), columns(ylo_at, zpos)]
        return to_mp(ref, ref, y_send.at[n], y_recv.at[n], y_other)

    def begin(n):
        y_copy(n, ylo).start()
        for direction in (0, 1):
            z_copy(n, 0, 1, direction).start()

    def kv_rows(owner, n, shift=0, count=part):
        return kv.at[pl.ds(pl.multiple_of(owner * rows + n * part + shift, 16), count), :]

    def q_rows(which, n):
        return qs.at[which, pl.ds(pl.multiple_of(n * part, 16), part), :]

    def out_copies(n):
        at = pl.ds(pl.multiple_of(n * part, 16), part)
        return (
            to_ctx(kv_out.at[at, :], kv_rows(me, n), h_send.at[n * 2], h_recv.at[n * 2], opposite),
            to_ctx(
                q_out.at[at, :], q_rows(0, n), h_send.at[n * 2 + 1], h_recv.at[n * 2 + 1], opposite
            ),
        )

    def out_waits(n):
        at = pl.ds(pl.multiple_of(n * part, 16), part)
        to_ctx(
            kv_out.at[at, :], kv_rows(opposite, n), h_send.at[n * 2], h_recv.at[n * 2], opposite
        ).wait_recv()
        to_ctx(
            q_out.at[at, :], q_rows(0, n), h_send.at[n * 2 + 1], h_recv.at[n * 2 + 1], opposite
        ).wait_recv()

    def across(owner):
        return (owner + 8) % CTX

    def ring_part(n, which, step, direction, outgoing):
        if step == 1:
            owner = me if outgoing else (x_left if direction == 0 else x_right)
            shift, count = 0, part
        else:
            near = x_left if direction == 0 else x_right
            owner = near if outgoing else x_far
            shift, count = direction * half, half
        if which == 1:
            owner = across(owner)
        ref = kv_rows(owner, n, shift, count)
        k = ((n * 2 + which) * 2 + step - 1) * 2 + direction
        target = x_right if direction == 0 else x_left
        return ref, to_ctx(ref, ref, r_send.at[k], r_recv.at[k], target)

    def core_part(n, kind, outgoing):
        if kind < 2:
            owner = me if outgoing else sibling
            if kind == 1:
                owner = across(owner)
            ref = kv_rows(owner, n)
        else:
            which, step, direction = (kind - 2) // 4, (kind - 2) // 2 % 2 + 1, (kind - 2) % 2
            near = x_left if direction == 0 else x_right
            owner = near if step == 1 else x_far
            if not outgoing:
                owner = owner + 1 - 2 * core
            if which == 1:
                owner = across(owner)
            ref = kv_rows(owner, n, *((0, part) if step == 1 else (direction * half, half)))
        k = n * 10 + kind
        return to_ctx(ref, ref, c_send.at[k], c_recv.at[k], sibling)

    def spread(n, which):
        core_part(n, which, True).start()
        for direction in (0, 1):
            ring_part(n, which, 1, direction, True)[1].start()

    def ring_tick(n, step):
        for which in (0, 1):
            for direction in (0, 1):
                ring_part(n, which, step, direction, False)[1].wait_recv()
                if step == 1:
                    ring_part(n, which, 2, direction, True)[1].start()
                core_part(n, 2 + which * 4 + (step - 1) * 2 + direction, True).start()

    own_head = yhi

    def project(n):
        at = pl.ds(pl.multiple_of(n * part, 16), part)
        wide = x[at, :].astype(jnp.float32)
        squares = jnp.sum(wide * wide, axis=1, keepdims=True)
        norm = lax.rsqrt(squares / all_chans + NORM_EPSILON)
        kv_at = pl.ds(pl.multiple_of(me * rows + n * part, 16), part)
        for j in range(3):
            scale = norm * (math.log2(math.e) / math.sqrt(HEAD_DIM)) if j == 0 else norm
            made = jnp.dot(x[at, :], w[j], preferred_element_type=jnp.float32) * scale
            made = made.astype(jnp.bfloat16)
            first, second = made[:, :HEAD_DIM], made[:, HEAD_DIM:]
            kept = jnp.where(own_head == 0, first, second)
            sent = jnp.where(own_head == 0, second, first)
            if j == 0:
                qs[1, at, :] = kept
                q_out[at, :] = sent
            else:
                lanes = slice((j - 1) * HEAD_DIM, j * HEAD_DIM)
                kv[kv_at, lanes] = kept
                kv_out[at, lanes] = sent

    begin(0)
    w_copy.wait()

    def one_chunk(n, carry):
        live, late = n < CHUNKS, n > 0

        @pl.when(live)
        def _():
            y_copy(n, 1 - ylo).wait_recv()
            for direction in (0, 1):
                z_copy(n, 1, 1, direction).start()

        for step in (1, 2, 3):

            @pl.when(live)
            def _(step=step):
                for plane in (0, 1):
                    for direction in (0, 1):
                        z_wait(n, plane, step, direction)
                        z_copy(n, plane, step + 1, direction).start()

            if step == 2:

                @pl.when(n + 1 < CHUNKS)
                def _():
                    begin(n + 1)

            @pl.when(late)
            def _(step=step):
                if step == 1:
                    out_waits(n - 1)
                    spread(n - 1, 1)
                else:
                    ring_tick(n - 1, step - 1)

        @pl.when(live)
        def _():
            for plane in (0, 1):
                for direction in (0, 1):
                    z_wait(n, plane, 4, direction)
            project(n)
            for copy in out_copies(n):
                copy.start()
            spread(n, 0)

        return carry

    lax.fori_loop(0, CHUNKS + 1, one_chunk, 0)

    def core_arrived(n, carry):
        for kind in range(10):
            core_part(n, kind, False).wait_recv()
        return carry

    lax.fori_loop(0, CHUNKS, core_arrived, 0)

    ones = jnp.ones((rows, HEAD_DIM), jnp.bfloat16)

    def attend(queries, key_at, shift):
        block = kv[pl.ds(pl.multiple_of(key_at, 16), rows), :]
        scores = lax.dot_general(
            queries, block[:, :HEAD_DIM], (((1,), (1,)), ((), ())),
            preferred_element_type=jnp.float32,
        )
        if shift is not None:
            row = lax.broadcasted_iota(jnp.int32, scores.shape, 0) + shift
            col = lax.broadcasted_iota(jnp.int32, scores.shape, 1)
            scores = jnp.where(col <= row, scores, NEG_FILL)
        old = q_max[...]
        new = jnp.maximum(old, jnp.max(scores, axis=1, keepdims=True))
        wide = jnp.concatenate([new] * (rows // 128), axis=1)
        weights = jnp.exp2(scores - wide).astype(jnp.bfloat16)
        values = jnp.concatenate([block[:, HEAD_DIM:], ones], axis=1)
        shrink = jnp.exp2(old - new)
        q_acc[...] = q_acc[...] * jnp.concatenate([shrink, shrink], axis=1) + jnp.dot(
            weights, values, preferred_element_type=jnp.float32
        )
        q_max[...] = new

    head_lanes = pl.ds(pl.multiple_of(own_head * HEAD_DIM, HEAD_DIM), HEAD_DIM)
    other_lanes = pl.ds(pl.multiple_of((1 - own_head) * HEAD_DIM, HEAD_DIM), HEAD_DIM)

    def attend_set(which, owner):
        for tile in range(rows // Q_TILE):
            at = slice(tile * Q_TILE, (tile + 1) * Q_TILE)
            q_acc[...] = jnp.zeros_like(q_acc)
            q_max[...] = jnp.full_like(q_max, NEG_FILL)

            def one_block(k, carry, at=at):
                attend(qs[which, at, :], k * rows, None)
                return carry

            lax.fori_loop(0, owner, one_block, 0)
            attend(qs[which, at, :], owner * rows, tile * Q_TILE)
            done = (q_acc[:, :HEAD_DIM] / q_acc[:, HEAD_DIM:]).astype(jnp.bfloat16)
            if which == 0:
                q_out[at, :] = done
            else:
                att[at, head_lanes] = done

    for n in range(CHUNKS):
        for copy in out_copies(n):
            copy.wait_send()
    attend_set(0, opposite)
    back = to_ctx(q_out, att.at[:, head_lanes], o_sem.at[0], o_sem.at[1], opposite)
    back.start()
    attend_set(1, me)
    to_ctx(q_out, att.at[:, other_lanes], o_sem.at[0], o_sem.at[1], opposite).wait_recv()
    att_copy = pltpu.make_async_copy(att, att_hbm, local_sem.at[3])
    att_copy.start()

    rim_copy.wait_send()
    for copy in state_copies:
        copy.wait_send()
    back.wait_send()

    def sent(n, carry):
        y_copy(n, ylo).wait_send()
        for direction in (0, 1):
            for plane in (0, 1):
                for step in (1, 2, 3, 4):
                    z_copy(n, plane, step, direction).wait_send()
            for which in (0, 1):
                for step in (1, 2):
                    ring_part(n, which, step, direction, True)[1].wait_send()
        for kind in range(10):
            core_part(n, kind, True).wait_send()
        return carry

    lax.fori_loop(0, CHUNKS, sent, 0)
    hyena_copy.wait()
    att_copy.wait()


def per_device(token_ids, feature_table, short_filter, rates, residues, skip_weight, w_qkv):
    rows = token_ids.shape[0]
    vocab, _, chans = feature_table.shape
    modes = rates.shape[1]
    all_chans, _, width = w_qkv.shape
    f32, bf16 = jnp.float32, jnp.bfloat16
    dma = pltpu.SemaphoreType.DMA
    vmem = pl.BlockSpec(memory_space=pltpu.VMEM)
    hbm = pl.BlockSpec(memory_space=pl.ANY)
    return pl.pallas_call(
        mixer_kernel,
        out_shape=(
            jax.ShapeDtypeStruct((rows, chans), bf16),
            jax.ShapeDtypeStruct((rows, width), bf16),
        ),
        in_specs=[vmem, hbm, vmem, vmem, vmem, vmem, hbm],
        out_specs=(hbm, hbm),
        scratch_shapes=[
            pltpu.VMEM((3, vocab, chans), bf16),
            pltpu.VMEM((3, all_chans, width), bf16),
            pltpu.VMEM((3, 8 + rows, chans), f32),
            pltpu.VMEM((chans // 128, rows, 128), f32),
            pltpu.VMEM((chans // 128, rows, 128), f32),
            pltpu.VMEM((1, 128), jnp.int32),
            pltpu.VMEM((modes, SEGS, chans), f32),
            pltpu.VMEM((modes, SEGS, chans), f32),
            pltpu.VMEM((modes, SEGS, chans), f32),
            pltpu.VMEM((modes, SEGS, chans), f32),
            pltpu.VMEM((CTX, modes, chans), f32),
            pltpu.VMEM((rows, all_chans), bf16),
            pltpu.VMEM((CTX * rows, 2 * HEAD_DIM), bf16),
            pltpu.VMEM((2, rows, HEAD_DIM), bf16),
            pltpu.VMEM((rows, 2 * HEAD_DIM), bf16),
            pltpu.VMEM((rows, HEAD_DIM), bf16),
            pltpu.VMEM((Q_TILE, 2 * HEAD_DIM), f32),
            pltpu.VMEM((Q_TILE, HEAD_DIM), f32),
            pltpu.VMEM((rows, width), bf16),
            dma((4,)),
            dma((2,)),
            dma((CTX - 1,)),
            dma((CTX - 1,)),
            dma((CHUNKS,)),
            dma((CHUNKS,)),
            dma((CHUNKS * 16,)),
            dma((CHUNKS * 16,)),
            dma((CHUNKS * 2,)),
            dma((CHUNKS * 2,)),
            dma((CHUNKS * 10,)),
            dma((CHUNKS * 10,)),
            dma((CHUNKS * 8,)),
            dma((CHUNKS * 8,)),
            dma((2,)),
        ],
        compiler_params=pltpu.CompilerParams(
            collective_id=0, has_side_effects=True, vmem_limit_bytes=56 * 1024 * 1024
        ),
        name="mixer",
    )(
        token_ids.reshape(1, rows),
        jnp.transpose(feature_table, (1, 0, 2)),
        short_filter,
        rates.T,
        residues.T,
        skip_weight.reshape(1, chans),
        jnp.transpose(w_qkv, (1, 0, 2)),
    )


def solution(mesh):
    in_specs = (
        P("ctx"),
        P(None, None, "mp"),
        P(None, None, "mp"),
        P("mp", None),
        P("mp", None),
        P("mp"),
        P(None, None, "mp"),
    )
    out_specs = (P("ctx", "mp"), P("ctx", "mp"))
    return jax.shard_map(
        per_device, mesh=mesh, in_specs=in_specs, out_specs=out_specs, check_vma=False
    )
```

```python
import functools
import math

import jax
import jax.numpy as jnp
from jax import lax
from jax.experimental import pallas as pl
from jax.experimental.pallas import tpu as pltpu
from jax.sharding import PartitionSpec as P

MESH = pl.DeviceIdType.MESH
HEAD_DIM = 128
TAPS = 3
SEGS = 8
NEG_FILL = -1e30
NORM_EPSILON = 1e-06

CTX = 16
MP = 16
PLANE = 8
CHUNKS = 4


def mixer_kernel(
    ids_ref, table_hbm, filt_ref, rates_ref, resid_ref, skip_ref, w_hbm,
    hyena_hbm, att_hbm,
    table, w, feats, gate, lead, rim, decay, weight, ends, starts, states,
    own, x, kv, qs, kv_out, q_out, q_acc, q_max, o_out, att,
    local_sem, rim_sem, state_send, state_recv,
    wy_send, wy_recv, wx_send, wx_recv,
    y_send, y_recv, z_send, z_recv, d_send, d_recv,
    h_send, h_recv, l_sem, c_send, c_recv, r_send, r_recv, o_send, o_recv,
):
    rows = feats.shape[1] - 8
    chans = feats.shape[2]
    modes = decay.shape[0]
    steps = rows // SEGS
    part = rows // CHUNKS
    half = part // 2
    all_chans = x.shape[1]
    total_len = CTX * rows
    span = CTX * part

    me = lax.axis_index("ctx")
    mp = lax.axis_index("mp")
    core = me % 2
    xpos = (me // 2) % 4
    yhi = me // 8
    zpos = mp % PLANE
    ylo = mp // PLANE
    sibling = me + 1 - 2 * core
    opposite = (me + 8) % CTX
    x_right = yhi * 8 + 2 * ((xpos + 1) % 4) + core
    x_left = yhi * 8 + 2 * ((xpos + 3) % 4) + core
    z_right = ylo * PLANE + (zpos + 1) % PLANE
    z_left = ylo * PLANE + (zpos + PLANE - 1) % PLANE
    y_other = (1 - ylo) * PLANE + zpos
    same = ylo == core
    crossed = ylo != core

    def remote(src, dst, send, recv, **target):
        return pltpu.make_async_remote_copy(
            src_ref=src, dst_ref=dst, send_sem=send, recv_sem=recv,
            device_id=target, device_id_type=MESH,
        )

    table_copy = pltpu.make_async_copy(table_hbm, table, local_sem.at[0])
    table_copy.start()
    w_copy = pltpu.make_async_copy(w_hbm, w, local_sem.at[1])

    @pl.when(same)
    def _():
        w_copy.start()

    barrier = pltpu.get_barrier_semaphore()
    for k in range(1, CTX):
        pl.semaphore_signal(
            barrier, inc=1, device_id={"ctx": (me + k) % CTX}, device_id_type=MESH
        )
    for other in (z_right, z_left):
        pl.semaphore_signal(barrier, inc=1, device_id={"mp": other}, device_id_type=MESH)
    for other in (sibling, (sibling + 8) % CTX):
        pl.semaphore_signal(
            barrier, inc=1, device_id={"ctx": other, "mp": y_other}, device_id_type=MESH
        )
    pl.semaphore_wait(barrier, CTX - 1 + 4)

    rim_copy = remote(
        ids_ref.at[:, pl.ds(rows - 128, 128)], rim, rim_sem.at[0], rim_sem.at[1],
        ctx=(me + 1) % CTX,
    )
    rim_copy.start()

    quarter = all_chans // 4

    def w_rows(j, place, shift=0, count=quarter):
        return w.at[j, pl.ds(pl.multiple_of((place % 4) * quarter + shift, 16), count), :]

    def wy_copy(j):
        at = pl.ds(pl.multiple_of(xpos * quarter, 16), quarter)
        return remote(
            w_hbm.at[j, at, :], w_rows(j, xpos), wy_send.at[j], wy_recv.at[j],
            ctx=sibling, mp=y_other,
        )

    def wx_copy(j, step, direction, outgoing):
        sign = 3 if direction == 0 else 1
        place = xpos + sign * (step - 1 if outgoing else step)
        ref = w_rows(j, place, *((0, quarter) if step == 1 else (direction * quarter // 2, quarter // 2)))
        k = (j * 2 + step - 1) * 2 + direction
        return remote(
            ref, ref, wx_send.at[k], wx_recv.at[k], ctx=x_right if direction == 0 else x_left
        )

    def w_tick(j, step):
        @pl.when(crossed)
        def _():
            if step == 0:
                wy_copy(j).wait_recv()
            for direction in (0, 1):
                if step > 0:
                    wx_copy(j, step, direction, False).wait_recv()
                if step < 2:
                    wx_copy(j, step + 1, direction, True).start()

    @pl.when(crossed)
    def _():
        for j in range(3):
            wy_copy(j).start()

    vocab = table.shape[1]

    def looked(ids, feature):
        at = lax.broadcasted_iota(jnp.int32, (vocab, ids.shape[1]), 0)
        hot = (at == ids).astype(jnp.float32).astype(jnp.bfloat16)
        return lax.dot_general(
            hot, table[feature], (((0,), (0,)), ((), ())), preferred_element_type=jnp.float32
        )

    damping = rates_ref[...] / total_len
    twice = 2.0 * damping
    small = twice * (
        1.0
        - twice
        * (
            0.5
            - twice
            * (1.0 / 6 - twice * (1.0 / 24 - twice * (1.0 / 120 - twice * (1.0 / 720))))
        )
    )
    grown = jnp.where(twice < 0.1, small, 1.0 - jnp.exp(-twice))
    mode_weight = resid_ref[...] * jnp.sqrt(grown)
    one_step = jnp.exp(-damping)
    for r in range(modes):
        decay[r] = jnp.broadcast_to(one_step[r : r + 1, :], (SEGS, chans))
        weight[r] = jnp.broadcast_to(mode_weight[r : r + 1, :], (SEGS, chans))

    table_copy.wait()
    for j in range(3):
        feats[j, 8:, :] = looked(ids_ref[...], j)
    rim_copy.wait_recv()
    for j in range(3):
        before = looked(rim[...], j)[120:128, :]
        feats[j, 0:8, :] = jnp.where(me > 0, before, 0.0)

    def smooth(j, at, count):
        total = filt_ref[0, j : j + 1, :] * feats[j, 8 + at : 8 + at + count, :]
        for tap in range(1, TAPS):
            total = total + filt_ref[tap, j : j + 1, :] * feats[
                j, 8 + at - tap : 8 + at - tap + count, :
            ]
        return total

    groups = [(g, slice(g * 128, (g + 1) * 128)) for g in range(chans // 128)]
    for at in range(0, rows, 96):
        gated = smooth(1, at, 96) * smooth(2, at, 96)
        led = smooth(0, at, 96)
        for g, lanes in groups:
            gate[g, at : at + 96, :] = gated[:, lanes]
            lead[g, at : at + 96, :] = led[:, lanes]

    for g, lanes in groups:
        fade = decay[:, :, lanes]

        def ended(i, state, g=g, fade=fade):
            row = gate[g, pl.ds(i, SEGS, stride=steps), :]
            return fade * state + row[None]

        ends[:, :, lanes] = lax.fori_loop(
            0, steps, ended, jnp.zeros((modes, SEGS, 128), jnp.float32)
        )
    segment_fade = jnp.exp(-damping * steps)
    running = jnp.zeros((modes, chans), jnp.float32)
    for j in range(SEGS):
        starts[:, j, :] = running
        running = segment_fade * running + ends[:, j, :]
    states[me] = running
    state_copies = []
    for k in range(1, CTX):
        copy = remote(
            states.at[me], states.at[me], state_send.at[k - 1], state_recv.at[k - 1],
            ctx=(me + k) % CTX,
        )
        copy.start()
        state_copies.append(copy)
    w_tick(0, 0)
    q_acc[...] = jnp.zeros_like(q_acc)
    q_max[...] = jnp.full_like(q_max, NEG_FILL)
    for k in range(1, CTX):
        source = (me + CTX - k) % CTX
        remote(
            states.at[source], states.at[source], state_send.at[k - 1], state_recv.at[k - 1],
            ctx=(me + k) % CTX,
        ).wait_recv()

    def gathered(k, total):
        gap = jnp.maximum(me - 1 - k, 0).astype(jnp.float32) * rows
        return total + jnp.where(k < me, jnp.exp(-damping * gap) * states[k], 0.0)

    incoming = lax.fori_loop(0, CTX, gathered, jnp.zeros((modes, chans), jnp.float32))
    for j in range(SEGS):
        starts[:, j, :] += jnp.exp(-damping * (steps * j)) * incoming
    w_tick(1, 0)

    for g, lanes in groups:
        fade = decay[:, :, lanes]
        skip = skip_ref[:, lanes]

        def stepped(i, state, g=g, lanes=lanes, fade=fade, skip=skip):
            at = pl.ds(i, SEGS, stride=steps)
            row = gate[g, at, :]
            state = fade * state + row[None]
            conv = jnp.sum(weight[:, :, lanes] * state, axis=0)
            gate[g, at, :] = lead[g, at, :] * (conv + skip * row)
            return state

        lax.fori_loop(0, steps, stepped, starts[:, :, lanes])
        if g == 0:
            w_tick(2, 0)
            w_tick(0, 1)

    def columns(plane, z_at):
        return pl.ds(pl.multiple_of((plane * PLANE + z_at) * chans, chans), chans)

    made_out = jnp.concatenate([gate[g] for g, _ in groups], axis=1).astype(jnp.bfloat16)
    own[...] = made_out

    @pl.when(same)
    def _():
        x[:, columns(ylo, zpos)] = own[...]

    def rows_of(n, shift=0, count=part):
        return pl.ds(pl.multiple_of(n * part + shift, 16), count)

    def y_copy(n):
        return remote(
            own.at[rows_of(n), :], x.at[rows_of(n), columns(ylo, zpos)],
            y_send.at[n], y_recv.at[n], ctx=sibling, mp=y_other,
        )

    @pl.when(crossed)
    def _():
        for n in range(CHUNKS):
            y_copy(n).start()

    hyena_copy = pltpu.make_async_copy(own, hyena_hbm, local_sem.at[2])
    hyena_copy.start()

    def z_part(n, step, direction, plane, outgoing):
        away = step - 1 if outgoing else step
        origin = (zpos + PLANE - away) % PLANE if direction == 0 else (zpos + away) % PLANE
        count, shift = (half, direction * half) if step == 4 else (part, 0)
        return x.at[rows_of(n, shift, count), columns(plane, origin)]

    def z_copy(n, step, direction, outgoing):
        ref = z_part(n, step, direction, core, outgoing)
        k = (n * 4 + step - 1) * 2 + direction
        return remote(
            ref, ref, z_send.at[k], z_recv.at[k], mp=z_right if direction == 0 else z_left
        )

    def d_copy(n, step, direction, outgoing):
        plane = core if outgoing else 1 - core
        if step == 0:
            ref = x.at[rows_of(n), columns(plane, zpos)]
        else:
            ref = z_part(n, step, direction, plane, False)
        k = n * 9 + (0 if step == 0 else 2 * step - 1 + direction)
        return remote(ref, ref, d_send.at[k], d_recv.at[k], ctx=sibling)

    d_kinds = [(0, 0)] + [(step, direction) for step in (1, 2, 3, 4) for direction in (0, 1)]

    def begin(n):
        @pl.when(crossed)
        def _():
            y_copy(n).wait_recv()

        for direction in (0, 1):
            z_copy(n, 1, direction, True).start()
        d_copy(n, 0, 0, True).start()

    def arrive(n, step):
        for direction in (0, 1):
            z_copy(n, step, direction, False).wait_recv()
            if step < 4:
                z_copy(n, step + 1, direction, True).start()
            d_copy(n, step, direction, True).start()

    def block_of(which, place, at_core):
        return which * 8 + 2 * (place % 4) + at_core

    def kv_rows(owner, n, shift=0, count=part):
        return kv.at[pl.ds(pl.multiple_of(n * span + owner * part + shift, 16), count), :]

    def home_copies(n, head):
        at = rows_of(n)
        k = (n * 2 + head) * 2
        r = (n * 2 + yhi) * 2
        target = {"ctx": block_of(head, xpos, ylo), "mp": core * PLANE + zpos}
        return (
            remote(
                kv_out.at[head, at, :], kv_rows(block_of(yhi, xpos, ylo), n),
                h_send.at[k], h_recv.at[r], **target,
            ),
            remote(
                q_out.at[head, at, :], qs.at[yhi, at, :],
                h_send.at[k + 1], h_recv.at[r + 1], **target,
            ),
        )

    def local_copies(n, head):
        at = rows_of(n)
        return (
            pltpu.make_async_copy(
                kv_out.at[head, at, :], kv_rows(block_of(yhi, xpos, ylo), n), l_sem.at[n * 2]
            ),
            pltpu.make_async_copy(
                q_out.at[head, at, :], qs.at[yhi, at, :], l_sem.at[n * 2 + 1]
            ),
        )

    def home_waits(n, which):
        at = rows_of(n)
        k = (n * 2 + which) * 2
        at_home = jnp.logical_and(same, yhi == which)

        @pl.when(at_home)
        def _():
            for copy in local_copies(n, which):
                copy.wait()

        @pl.when(jnp.logical_not(at_home))
        def _():
            target = {"ctx": block_of(which, xpos, ylo), "mp": core * PLANE + zpos}
            remote(
                kv_out.at[0, at, :], kv_rows(block_of(which, xpos, core), n),
                h_send.at[k], h_recv.at[k], **target,
            ).wait_recv()
            remote(
                q_out.at[0, at, :], qs.at[which, at, :], h_send.at[k + 1], h_recv.at[k + 1],
                **target,
            ).wait_recv()

    def ring_part(n, which, step, direction, at_core, outgoing):
        sign = 3 if direction == 0 else 1
        away = step - 1 if outgoing else step
        owner = block_of(which, xpos + sign * away, at_core)
        return kv_rows(owner, n, *((0, part) if step == 1 else (direction * half, half)))

    def ring_copy(n, which, step, direction, outgoing):
        ref = ring_part(n, which, step, direction, core, outgoing)
        k = ((n * 2 + which) * 2 + step - 1) * 2 + direction
        return remote(
            ref, ref, r_send.at[k], r_recv.at[k], ctx=x_right if direction == 0 else x_left
        )

    def core_copy(n, which, step, direction, outgoing):
        at_core = core if outgoing else 1 - core
        if step == 0:
            ref = kv_rows(block_of(which, xpos, at_core), n)
        else:
            ref = ring_part(n, which, step, direction, at_core, False)
        k = (n * 2 + which) * 5 + (0 if step == 0 else 2 * step - 1 + direction)
        return remote(ref, ref, c_send.at[k], c_recv.at[k], ctx=sibling)

    c_kinds = [(0, 0)] + [(step, direction) for step in (1, 2) for direction in (0, 1)]

    def ring_begin(n):
        for which in (0, 1):
            home_waits(n, which)
            for direction in (0, 1):
                ring_copy(n, which, 1, direction, True).start()
            core_copy(n, which, 0, 0, True).start()

    def ring_tick(n, step):
        for which in (0, 1):
            for direction in (0, 1):
                ring_copy(n, which, step, direction, False).wait_recv()
                if step == 1:
                    ring_copy(n, which, 2, direction, True).start()
                core_copy(n, which, step, direction, True).start()

    def ring_end(n):
        for which in (0, 1):
            for kind in c_kinds:
                core_copy(n, which, *kind, False).wait_recv()

    def project(n):
        for kind in d_kinds:
            d_copy(n, *kind, False).wait_recv()
        at = rows_of(n)
        wide = x[at, :].astype(jnp.float32)
        squares = jnp.sum(wide * wide, axis=1, keepdims=True)
        norm = lax.rsqrt(squares / all_chans + NORM_EPSILON)
        for j in range(3):
            scale = norm * (math.log2(math.e) / math.sqrt(HEAD_DIM)) if j == 0 else norm
            made = jnp.dot(x[at, :], w[j], preferred_element_type=jnp.float32) * scale
            made = made.astype(jnp.bfloat16)
            for head in (0, 1):
                piece = made[:, head * HEAD_DIM : (head + 1) * HEAD_DIM]
                if j == 0:
                    q_out[head, at, :] = piece
                else:
                    kv_out[head, at, (j - 1) * HEAD_DIM : j * HEAD_DIM] = piece
        for head in (0, 1):
            stays = jnp.logical_and(same, yhi == head)

            @pl.when(stays)
            def _(head=head):
                for copy in local_copies(n, head):
                    copy.start()

            @pl.when(jnp.logical_not(stays))
            def _(head=head):
                for copy in home_copies(n, head):
                    copy.start()

    ones = jnp.ones((span // 2, HEAD_DIM), jnp.bfloat16)

    def scores_of(queries, block):
        return lax.dot_general(
            queries, block[:, :HEAD_DIM], (((1,), (1,)), ((), ())),
            preferred_element_type=jnp.float32,
        )

    def masked(scores, bound):
        col = lax.broadcasted_iota(jnp.int32, scores.shape, 1)
        return jnp.where(col < bound, scores, NEG_FILL)

    def pair(q_chunk, k_chunk):
        at = rows_of(q_chunk)
        row = lax.broadcasted_iota(jnp.int32, (part, 1), 0) + 1
        extra = jnp.where(k_chunk < q_chunk, part, jnp.where(k_chunk == q_chunk, row, 0))
        bound = (2 * xpos + core) * part + extra
        base = pl.multiple_of(k_chunk * span, 16)
        low = kv[pl.ds(base, span // 2), :]
        high = kv[pl.ds(pl.multiple_of(base + span // 2, 16), span // 2), :]
        for which in (1, 0):
            queries = qs[which, at, :]
            if which == 1:
                blocks = [low, high]
                scores = [scores_of(queries, low), masked(scores_of(queries, high), bound)]
            else:
                blocks = [low]
                scores = [masked(scores_of(queries, low), bound)]
            old = q_max[which, at, :]
            new = old
            for s in scores:
                new = jnp.maximum(new, jnp.max(s, axis=1, keepdims=True))
            wide = jnp.concatenate([new] * (span // 256), axis=1)
            shrink = jnp.exp2(old - new)
            total = q_acc[which, at, :] * jnp.concatenate([shrink, shrink], axis=1)
            for s, block in zip(scores, blocks):
                weights = jnp.exp2(s - wide).astype(jnp.bfloat16)
                values = jnp.concatenate([block[:, HEAD_DIM:], ones], axis=1)
                total = total + jnp.dot(weights, values, preferred_element_type=jnp.float32)
            q_acc[which, at, :] = total
            q_max[which, at, :] = new

    def pairs(n, first, last):
        def one(i, carry):
            q_chunk = jnp.where(i < n, i, n)
            k_chunk = jnp.where(i < n, n, jnp.where(i < 2 * n, i - n, n))
            pair(q_chunk, k_chunk)
            return carry

        lax.fori_loop(first, last, one, 0)

    head_lanes = pl.ds(pl.multiple_of(yhi * HEAD_DIM, HEAD_DIM), HEAD_DIM)
    other_lanes = pl.ds(pl.multiple_of((1 - yhi) * HEAD_DIM, HEAD_DIM), HEAD_DIM)

    def o_copy(m, lanes):
        at = rows_of(m)
        return remote(
            o_out.at[1 - yhi, at, :], att.at[at, lanes], o_send.at[m], o_recv.at[m], ctx=opposite
        )

    def finish(m):
        at = rows_of(m)
        for which in (0, 1):
            done = q_acc[which, at, :HEAD_DIM] / q_acc[which, at, HEAD_DIM:]
            o_out[which, at, :] = done.astype(jnp.bfloat16)
        o_copy(m, head_lanes).start()
        att[at, head_lanes] = o_out[yhi, at, :]

    w_tick(1, 1)

    def round_of(it, carry):
        def when(n):
            return pl.when(jnp.logical_and(n >= 0, n < CHUNKS))

        def some_pairs(n, piece):
            @pl.when(jnp.logical_and(n >= 0, n < CHUNKS - 1))
            def _():
                count = 2 * n + 1
                pairs(n, count * piece // 3, count * (piece + 1) // 3)

        @when(it)
        def _():
            begin(it)

        @when(it - 2)
        def _():
            arrive(it - 2, 2)

        @when(it - 1)
        def _():
            arrive(it - 1, 1)

        @pl.when(it == 1)
        def _():
            w_tick(2, 1)

        @pl.when(it == 2)
        def _():
            w_tick(0, 2)

        some_pairs(it - 7, 2)

        @when(it - 6)
        def _():
            ring_end(it - 6)

        some_pairs(it - 6, 0)

        @when(it - 5)
        def _():
            ring_tick(it - 5, 1)

        @when(it - 3)
        def _():
            arrive(it - 3, 4)

        some_pairs(it - 6, 1)

        @when(it - 4)
        def _():
            ring_begin(it - 4)

        @pl.when(it == 3)
        def _():
            w_tick(1, 2)
            w_tick(2, 2)

            @pl.when(same)
            def _():
                w_copy.wait()

        @when(it - 3)
        def _():
            project(it - 3)

        @when(it - 5)
        def _():
            ring_tick(it - 5, 2)

        @when(it - 2)
        def _():
            arrive(it - 2, 3)

        return carry

    lax.fori_loop(0, CHUNKS + 6, round_of, 0)

    last = CHUNKS - 1

    def closing(m, carry):
        pair(m, last)
        finish(m)
        return carry

    lax.fori_loop(0, last, closing, 0)
    pairs(last, last, 2 * last + 1)
    finish(last)

    rim_copy.wait_send()
    for copy in state_copies:
        copy.wait_send()

    @pl.when(crossed)
    def _():
        for j in range(3):
            wy_copy(j).wait_send()
            for step in (1, 2):
                for direction in (0, 1):
                    wx_copy(j, step, direction, True).wait_send()

    def sent(n, carry):
        @pl.when(crossed)
        def _():
            y_copy(n).wait_send()

        for direction in (0, 1):
            for step in (1, 2, 3, 4):
                z_copy(n, step, direction, True).wait_send()
        for kind in d_kinds:
            d_copy(n, *kind, True).wait_send()
        for which in (0, 1):
            for step, direction in c_kinds:
                core_copy(n, which, step, direction, True).wait_send()
                if step > 0:
                    ring_copy(n, which, step, direction, True).wait_send()

            @pl.when(jnp.logical_not(jnp.logical_and(same, yhi == which)))
            def _(which=which):
                for copy in home_copies(n, which):
                    copy.wait_send()

        o_copy(n, head_lanes).wait_send()
        return carry

    lax.fori_loop(0, CHUNKS, sent, 0)
    hyena_copy.wait()
    for m in range(CHUNKS):
        o_copy(m, other_lanes).wait_recv()
    att_copy = pltpu.make_async_copy(att, att_hbm, local_sem.at[3])
    att_copy.start()
    att_copy.wait()


def per_device(token_ids, feature_table, short_filter, rates, residues, skip_weight, w_qkv):
    rows = token_ids.shape[0]
    vocab, _, chans = feature_table.shape
    modes = rates.shape[1]
    all_chans, _, width = w_qkv.shape
    f32, bf16 = jnp.float32, jnp.bfloat16
    dma = pltpu.SemaphoreType.DMA
    vmem = pl.BlockSpec(memory_space=pltpu.VMEM)
    hbm = pl.BlockSpec(memory_space=pl.ANY)
    return pl.pallas_call(
        mixer_kernel,
        out_shape=(
            jax.ShapeDtypeStruct((rows, chans), bf16),
            jax.ShapeDtypeStruct((rows, width), bf16),
        ),
        in_specs=[vmem, hbm, vmem, vmem, vmem, vmem, hbm],
        out_specs=(hbm, hbm),
        scratch_shapes=[
            pltpu.VMEM((3, vocab, chans), bf16),
            pltpu.VMEM((3, all_chans, width), bf16),
            pltpu.VMEM((3, 8 + rows, chans), f32),
            pltpu.VMEM((chans // 128, rows, 128), f32),
            pltpu.VMEM((chans // 128, rows, 128), f32),
            pltpu.VMEM((1, 128), jnp.int32),
            pltpu.VMEM((modes, SEGS, chans), f32),
            pltpu.VMEM((modes, SEGS, chans), f32),
            pltpu.VMEM((modes, SEGS, chans), f32),
            pltpu.VMEM((modes, SEGS, chans), f32),
            pltpu.VMEM((CTX, modes, chans), f32),
            pltpu.VMEM((rows, chans), bf16),
            pltpu.VMEM((rows, all_chans), bf16),
            pltpu.VMEM((CTX * rows, 2 * HEAD_DIM), bf16),
            pltpu.VMEM((2, rows, HEAD_DIM), bf16),
            pltpu.VMEM((2, rows, 2 * HEAD_DIM), bf16),
            pltpu.VMEM((2, rows, HEAD_DIM), bf16),
            pltpu.VMEM((2, rows, 2 * HEAD_DIM), f32),
            pltpu.VMEM((2, rows, HEAD_DIM), f32),
            pltpu.VMEM((2, rows, HEAD_DIM), bf16),
            pltpu.VMEM((rows, width), bf16),
            dma((4,)),
            dma((2,)),
            dma((CTX - 1,)),
            dma((CTX - 1,)),
            dma((3,)),
            dma((3,)),
            dma((12,)),
            dma((12,)),
            dma((CHUNKS,)),
            dma((CHUNKS,)),
            dma((CHUNKS * 8,)),
            dma((CHUNKS * 8,)),
            dma((CHUNKS * 9,)),
            dma((CHUNKS * 9,)),
            dma((CHUNKS * 4,)),
            dma((CHUNKS * 4,)),
            dma((CHUNKS * 2,)),
            dma((CHUNKS * 10,)),
            dma((CHUNKS * 10,)),
            dma((CHUNKS * 8,)),
            dma((CHUNKS * 8,)),
            dma((CHUNKS,)),
            dma((CHUNKS,)),
        ],
        compiler_params=pltpu.CompilerParams(
            collective_id=0, has_side_effects=True, vmem_limit_bytes=56 * 1024 * 1024
        ),
        name="mixer",
    )(
        token_ids.reshape(1, rows),
        jnp.transpose(feature_table, (1, 0, 2)),
        short_filter,
        rates.T,
        residues.T,
        skip_weight.reshape(1, chans),
        jnp.transpose(w_qkv, (1, 0, 2)),
    )


def solution(mesh):
    in_specs = (
        P("ctx"),
        P(None, None, "mp"),
        P(None, None, "mp"),
        P("mp", None),
        P("mp", None),
        P("mp"),
        P(None, None, "mp"),
    )
    out_specs = (P("ctx", "mp"), P("ctx", "mp"))
    return jax.shard_map(
        per_device, mesh=mesh, in_specs=in_specs, out_specs=out_specs, check_vma=False
    )
```

```python
import functools
import math

import jax
import jax.numpy as jnp
from jax import lax
from jax.experimental import pallas as pl
from jax.experimental.pallas import tpu as pltpu
from jax.sharding import PartitionSpec as P

MESH = pl.DeviceIdType.MESH
HEAD_DIM = 128
TAPS = 3
SEGS = 8
NEG_FILL = -1e30
NORM_EPSILON = 1e-06

CTX = 16
MP = 16
PLANE = 8
CHUNKS = 4


def mixer_kernel(
    ids_ref, table_hbm, filt_ref, rates_ref, resid_ref, skip_ref, w_hbm,
    hyena_hbm, att_hbm,
    table, hot, w, feats, gate, lead, mixed, rim, decay, weight, ends, starts, states,
    own, x, kv, qs, kv_out, q_out, q_acc, q_max, o_out, att,
    local_sem, rim_sem, state_send, state_recv,
    wy_send, wy_recv, wx_send, wx_recv,
    y_send, y_recv, z_send, z_recv, d_send, d_recv,
    h_send, h_recv, l_sem, c_send, c_recv, r_send, r_recv, o_send, o_recv,
):
    rows = feats.shape[1] - 8
    chans = feats.shape[2]
    modes = decay.shape[0]
    steps = rows // SEGS
    part = rows // CHUNKS
    half = part // 2
    all_chans = x.shape[1]
    total_len = CTX * rows
    span = CTX * part

    me = lax.axis_index("ctx")
    mp = lax.axis_index("mp")
    core = me % 2
    xpos = (me // 2) % 4
    yhi = me // 8
    zpos = mp % PLANE
    ylo = mp // PLANE
    sibling = me + 1 - 2 * core
    opposite = (me + 8) % CTX
    x_right = yhi * 8 + 2 * ((xpos + 1) % 4) + core
    x_left = yhi * 8 + 2 * ((xpos + 3) % 4) + core
    z_right = ylo * PLANE + (zpos + 1) % PLANE
    z_left = ylo * PLANE + (zpos + PLANE - 1) % PLANE
    y_other = (1 - ylo) * PLANE + zpos
    same = ylo == core
    crossed = ylo != core

    def remote(src, dst, send, recv, **target):
        return pltpu.make_async_remote_copy(
            src_ref=src, dst_ref=dst, send_sem=send, recv_sem=recv,
            device_id=target, device_id_type=MESH,
        )

    table_copy = pltpu.make_async_copy(table_hbm, table, local_sem.at[0])
    table_copy.start()
    w_copy = pltpu.make_async_copy(w_hbm, w, local_sem.at[1])

    @pl.when(same)
    def _():
        w_copy.start()

    barrier = pltpu.get_barrier_semaphore()
    for k in range(1, CTX):
        pl.semaphore_signal(
            barrier, inc=1, device_id={"ctx": (me + k) % CTX}, device_id_type=MESH
        )
    for other in (z_right, z_left):
        pl.semaphore_signal(barrier, inc=1, device_id={"mp": other}, device_id_type=MESH)
    for other in (sibling, (sibling + 8) % CTX):
        pl.semaphore_signal(
            barrier, inc=1, device_id={"ctx": other, "mp": y_other}, device_id_type=MESH
        )
    vocab = table.shape[1]
    place = lax.broadcasted_iota(jnp.int32, (128, 128), 1)

    def one_hot(ids_row):
        ids = jnp.transpose(jnp.broadcast_to(ids_row, (128, 128)))
        hits = [(ids == place + at).astype(jnp.float32) for at in range(0, vocab, 128)]
        return jnp.concatenate(hits, axis=1).astype(jnp.bfloat16)

    for r in range(rows // 128):
        hot[r * 128 : (r + 1) * 128, :] = one_hot(ids_ref[r : r + 1, :])
    table_copy.wait()
    for j in range(3):
        feats[j, 8:, :] = jnp.dot(hot[...], table[j], preferred_element_type=jnp.float32)

    pl.semaphore_wait(barrier, CTX - 1 + 4)

    rim_copy = remote(ids_ref, rim, rim_sem.at[0], rim_sem.at[1], ctx=(me + 1) % CTX)
    rim_copy.start()

    quarter = all_chans // 4
    piece = quarter // 2

    def w_rows(i, place, shift=0, count=piece):
        at = (place % 4) * quarter + (i % 2) * piece + shift
        return pl.ds(pl.multiple_of(at, 16), count)

    def wy_copy(i):
        at = w_rows(i, xpos)
        return remote(
            w_hbm.at[i // 2, at, :], w.at[i // 2, at, :], wy_send.at[i], wy_recv.at[i],
            ctx=sibling if i % 2 == 0 else (sibling + 8) % CTX, mp=y_other,
        )

    def wx_copy(i, step, direction, outgoing):
        sign = 3 if direction == 0 else 1
        away = sign * (step - 1 if outgoing else step)
        cut = (0, piece) if step == 1 else (direction * piece // 2, piece // 2)
        ref = w.at[i // 2, w_rows(i, xpos + away, *cut), :]
        k = (i * 2 + step - 1) * 2 + direction
        return remote(
            ref, ref, wx_send.at[k], wx_recv.at[k], ctx=x_right if direction == 0 else x_left
        )

    def w_ticks(*ticks):
        @pl.when(crossed)
        def _():
            for step, i in ticks:
                if step == 0:
                    wy_copy(i).wait_recv()
                for direction in (0, 1):
                    if step > 0:
                        wx_copy(i, step, direction, False).wait_recv()
                    if step < 2:
                        wx_copy(i, step + 1, direction, True).start()

    @pl.when(crossed)
    def _():
        for i in range(6):
            wy_copy(i).start()

    damping = rates_ref[...] / total_len
    twice = 2.0 * damping
    small = twice * (
        1.0
        - twice
        * (
            0.5
            - twice
            * (1.0 / 6 - twice * (1.0 / 24 - twice * (1.0 / 120 - twice * (1.0 / 720))))
        )
    )
    grown = jnp.where(twice < 0.1, small, 1.0 - jnp.exp(-twice))
    mode_weight = resid_ref[...] * jnp.sqrt(grown)
    one_step = jnp.exp(-damping)
    for r in range(modes):
        decay[r] = jnp.broadcast_to(one_step[r : r + 1, :], (SEGS, chans))
        weight[r] = jnp.broadcast_to(mode_weight[r : r + 1, :], (SEGS, chans))

    def smooth(j, at, count):
        total = filt_ref[0, j : j + 1, :] * feats[j, 8 + at : 8 + at + count, :]
        for tap in range(1, TAPS):
            total = total + filt_ref[tap, j : j + 1, :] * feats[
                j, 8 + at - tap : 8 + at - tap + count, :
            ]
        return total

    groups = [(g, slice(g * 128, (g + 1) * 128)) for g in range(chans // 128)]
    def smooth_all(at):
        gated = smooth(1, at, 96) * smooth(2, at, 96)
        led = smooth(0, at, 96)
        for g, lanes in groups:
            gate[g, at : at + 96, :] = gated[:, lanes]
            lead[g, at : at + 96, :] = led[:, lanes]

    for at in range(96, rows, 96):
        smooth_all(at)
    rim_copy.wait_recv()
    before_hot = one_hot(rim[rows // 128 - 1 : rows // 128, :])[112:128, :]
    for j in range(3):
        before = jnp.dot(before_hot, table[j], preferred_element_type=jnp.float32)[8:16, :]
        feats[j, 0:8, :] = jnp.where(me > 0, before, 0.0)
    smooth_all(0)

    for g, lanes in groups:
        fade = decay[:, :, lanes]

        def ended(i, state, g=g, fade=fade):
            row = gate[g, pl.ds(i, SEGS, stride=steps), :]
            return fade * state + row[None]

        ends[:, :, lanes] = lax.fori_loop(
            0, steps, ended, jnp.zeros((modes, SEGS, 128), jnp.float32), unroll=4
        )
    segment_fade = jnp.exp(-damping * steps)
    running = jnp.zeros((modes, chans), jnp.float32)
    for j in range(SEGS):
        starts[:, j, :] = running
        running = segment_fade * running + ends[:, j, :]
    states[me] = running

    def state_copy(k, owner):
        ref = states.at[owner]
        return remote(
            ref, ref, state_send.at[k - 1], state_recv.at[k - 1], ctx=(me + k) % CTX
        )

    for k in range(1, CTX):

        @pl.when(me + k < CTX)
        def _(k=k):
            state_copy(k, me).start()

    w_ticks((0, 0), (0, 1))
    q_acc[...] = jnp.zeros_like(q_acc)
    q_max[...] = jnp.full_like(q_max, NEG_FILL)
    for k in range(1, CTX):

        @pl.when(me >= k)
        def _(k=k):
            state_copy(k, (me + CTX - k) % CTX).wait_recv()

    def gathered(k, total):
        gap = (me - 1 - k).astype(jnp.float32) * rows
        return total + jnp.exp(-damping * gap) * states[k]

    incoming = lax.fori_loop(0, me, gathered, jnp.zeros((modes, chans), jnp.float32))
    for j in range(SEGS):
        starts[:, j, :] += jnp.exp(-damping * (steps * j)) * incoming
    w_ticks((0, 2), (0, 3))

    for g, lanes in groups:
        fade = decay[:, :, lanes]
        skip = skip_ref[:, lanes]

        def stepped(i, state, g=g, lanes=lanes, fade=fade, skip=skip):
            at = pl.ds(i, SEGS, stride=steps)
            row = gate[g, at, :]
            state = fade * state + row[None]
            conv = jnp.sum(weight[:, :, lanes] * state, axis=0)
            mixed[g, at, :] = lead[g, at, :] * (conv + skip * row)
            return state

        lax.fori_loop(0, steps, stepped, starts[:, :, lanes], unroll=2)

    def columns(plane, z_at):
        return pl.ds(pl.multiple_of((plane * PLANE + z_at) * chans, chans), chans)

    made_out = jnp.concatenate([mixed[g] for g, _ in groups], axis=1).astype(jnp.bfloat16)
    own[...] = made_out

    @pl.when(same)
    def _():
        x[:, columns(ylo, zpos)] = own[...]

    def rows_of(n, shift=0, count=part):
        return pl.ds(pl.multiple_of(n * part + shift, 16), count)

    def y_copy(n):
        return remote(
            own.at[rows_of(n), :], x.at[rows_of(n), columns(ylo, zpos)],
            y_send.at[n], y_recv.at[n], ctx=sibling, mp=y_other,
        )

    @pl.when(crossed)
    def _():
        for n in range(CHUNKS):
            y_copy(n).start()

    hyena_copy = pltpu.make_async_copy(own, hyena_hbm, local_sem.at[2])
    hyena_copy.start()
    w_ticks((1, 0))

    def z_part(n, step, direction, plane, outgoing):
        away = step - 1 if outgoing else step
        origin = (zpos + PLANE - away) % PLANE if direction == 0 else (zpos + away) % PLANE
        count, shift = (half, direction * half) if step == 4 else (part, 0)
        return x.at[rows_of(n, shift, count), columns(plane, origin)]

    def z_copy(n, step, direction, outgoing):
        ref = z_part(n, step, direction, core, outgoing)
        k = (n * 4 + step - 1) * 2 + direction
        return remote(
            ref, ref, z_send.at[k], z_recv.at[k], mp=z_right if direction == 0 else z_left
        )

    def d_copy(n, outgoing):
        plane = core if outgoing else 1 - core
        width = PLANE * chans
        ref = x.at[rows_of(n), pl.ds(pl.multiple_of(plane * width, width), width)]
        return remote(ref, ref, d_send.at[n], d_recv.at[n], ctx=sibling)

    def begin(n):
        @pl.when(crossed)
        def _():
            y_copy(n).wait_recv()

        for direction in (0, 1):
            z_copy(n, 1, direction, True).start()

    def arrive(n, step):
        for direction in (0, 1):
            z_copy(n, step, direction, False).wait_recv()
            if step < 4:
                z_copy(n, step + 1, direction, True).start()
        if step == 4:
            d_copy(n, True).start()

    def block_of(which, place, at_core):
        return which * 8 + 2 * place + at_core

    def kv_home(which, at_core, n):
        return kv.at[n, which, at_core, xpos]

    def home_copies(n, head):
        at = rows_of(n)
        k = (n * 2 + head) * 2
        r = (n * 2 + yhi) * 2
        target = {"ctx": block_of(head, xpos, ylo), "mp": core * PLANE + zpos}
        return (
            remote(
                kv_out.at[head, at, :], kv_home(yhi, ylo, n),
                h_send.at[k], h_recv.at[r], **target,
            ),
            remote(
                q_out.at[head, at, :], qs.at[yhi, at, :],
                h_send.at[k + 1], h_recv.at[r + 1], **target,
            ),
        )

    def local_copies(n, head):
        at = rows_of(n)
        return (
            pltpu.make_async_copy(
                kv_out.at[head, at, :], kv_home(yhi, ylo, n), l_sem.at[n * 2]
            ),
            pltpu.make_async_copy(
                q_out.at[head, at, :], qs.at[yhi, at, :], l_sem.at[n * 2 + 1]
            ),
        )

    def home_waits(n, which):
        at = rows_of(n)
        k = (n * 2 + which) * 2
        at_home = jnp.logical_and(same, yhi == which)

        @pl.when(at_home)
        def _():
            for copy in local_copies(n, which):
                copy.wait()

        @pl.when(jnp.logical_not(at_home))
        def _():
            target = {"ctx": block_of(which, xpos, ylo), "mp": core * PLANE + zpos}
            remote(
                kv_out.at[0, at, :], kv_home(which, core, n),
                h_send.at[k], h_recv.at[k], **target,
            ).wait_recv()
            remote(
                q_out.at[0, at, :], qs.at[which, at, :], h_send.at[k + 1], h_recv.at[k + 1],
                **target,
            ).wait_recv()

    def ring_copy(n, step, direction, outgoing):
        sign = 3 if direction == 0 else 1
        away = step - 1 if outgoing else step
        at = slice(0, part) if step == 1 else slice(direction * half, direction * half + half)
        ref = kv.at[n, :, core, (xpos + sign * away) % 4, at, :]
        k = (n * 2 + step - 1) * 2 + direction
        return remote(
            ref, ref, r_send.at[k], r_recv.at[k], ctx=x_right if direction == 0 else x_left
        )

    def core_copy(n, outgoing):
        ref = kv.at[n, :, core if outgoing else 1 - core]
        return remote(ref, ref, c_send.at[n], c_recv.at[n], ctx=sibling)

    def ring_begin(n):
        for which in (0, 1):
            home_waits(n, which)
        for direction in (0, 1):
            ring_copy(n, 1, direction, True).start()

    def ring_tick(n, step):
        for direction in (0, 1):
            ring_copy(n, step, direction, False).wait_recv()
            if step == 1:
                ring_copy(n, 2, direction, True).start()
        if step == 2:
            core_copy(n, True).start()

    def ring_end(n):
        core_copy(n, False).wait_recv()

    def project(n):
        d_copy(n, False).wait_recv()
        at = rows_of(n)
        wide = x[at, :].astype(jnp.float32)
        squares = jnp.sum(wide * wide, axis=1, keepdims=True)
        norm = lax.rsqrt(squares / all_chans + NORM_EPSILON)
        for j in range(3):
            scale = norm * (math.log2(math.e) / math.sqrt(HEAD_DIM)) if j == 0 else norm
            made = jnp.dot(x[at, :], w[j], preferred_element_type=jnp.float32) * scale
            made = made.astype(jnp.bfloat16)
            for head in (0, 1):
                piece = made[:, head * HEAD_DIM : (head + 1) * HEAD_DIM]
                if j == 0:
                    q_out[head, at, :] = piece
                else:
                    kv_out[head, at, (j - 1) * HEAD_DIM : j * HEAD_DIM] = piece
        for head in (0, 1):
            stays = jnp.logical_and(same, yhi == head)

            @pl.when(stays)
            def _(head=head):
                for copy in local_copies(n, head):
                    copy.start()

            @pl.when(jnp.logical_not(stays))
            def _(head=head):
                for copy in home_copies(n, head):
                    copy.start()

    ones = jnp.ones((span // 2, HEAD_DIM), jnp.bfloat16)

    def scores_of(queries, block):
        return lax.dot_general(
            queries, block[:, :HEAD_DIM], (((1,), (1,)), ((), ())),
            preferred_element_type=jnp.float32,
        )

    def masked(scores, bounds):
        width = scores.shape[1] // 2
        col = lax.broadcasted_iota(jnp.int32, (part, width), 1)
        return jnp.concatenate(
            [
                jnp.where(col < bound, scores[:, i * width : (i + 1) * width], NEG_FILL)
                for i, bound in enumerate(bounds)
            ],
            axis=1,
        )

    def pair(q_chunk, k_chunk):
        at = rows_of(q_chunk)
        row = lax.broadcasted_iota(jnp.int32, (part, 1), 0) + 1
        extra = jnp.where(k_chunk < q_chunk, part, jnp.where(k_chunk == q_chunk, row, 0))
        bounds = [
            xpos * part + jnp.where(core == 0, extra, part),
            xpos * part + jnp.where(core == 0, 0, extra),
        ]
        low = kv[k_chunk, 0].reshape(span // 2, 2 * HEAD_DIM)
        high = kv[k_chunk, 1].reshape(span // 2, 2 * HEAD_DIM)
        for which in (1, 0):
            queries = qs[which, at, :]
            if which == 1:
                blocks = [low, high]
                scores = [scores_of(queries, low), masked(scores_of(queries, high), bounds)]
            else:
                blocks = [low]
                scores = [masked(scores_of(queries, low), bounds)]
            old = q_max[which, at, :]
            new = old
            for s in scores:
                new = jnp.maximum(new, jnp.max(s, axis=1, keepdims=True))
            wide = jnp.concatenate([new] * (span // 256), axis=1)
            shrink = jnp.exp2(old - new)
            total = q_acc[which, at, :] * jnp.concatenate([shrink, shrink], axis=1)
            for s, block in zip(scores, blocks):
                weights = jnp.exp2(s - wide).astype(jnp.bfloat16)
                values = jnp.concatenate([block[:, HEAD_DIM:], ones], axis=1)
                total = total + jnp.dot(weights, values, preferred_element_type=jnp.float32)
            q_acc[which, at, :] = total
            q_max[which, at, :] = new

    def pairs(n, first, last):
        def one(i, carry):
            q_chunk = jnp.where(i < n, i, n)
            k_chunk = jnp.where(i < n, n, jnp.where(i < 2 * n, i - n, n))
            pair(q_chunk, k_chunk)
            return carry

        lax.fori_loop(first, last, one, 0)

    head_lanes = pl.ds(pl.multiple_of(yhi * HEAD_DIM, HEAD_DIM), HEAD_DIM)
    other_lanes = pl.ds(pl.multiple_of((1 - yhi) * HEAD_DIM, HEAD_DIM), HEAD_DIM)

    def o_copy(m, lanes):
        at = rows_of(m)
        return remote(
            o_out.at[1 - yhi, at, :], att.at[at, lanes], o_send.at[m], o_recv.at[m], ctx=opposite
        )

    def finish(m):
        at = rows_of(m)
        for which in (0, 1):
            done = q_acc[which, at, :HEAD_DIM] / q_acc[which, at, HEAD_DIM:]
            o_out[which, at, :] = done.astype(jnp.bfloat16)
        o_copy(m, head_lanes).start()
        att[at, head_lanes] = o_out[yhi, at, :]

    def round_of(it, carry):
        def when(n):
            return pl.when(jnp.logical_and(n >= 0, n < CHUNKS))

        def some_pairs(n, piece):
            @pl.when(jnp.logical_and(n >= 0, n < CHUNKS - 1))
            def _():
                count = 2 * n + 1
                pairs(n, count * piece // 3, count * (piece + 1) // 3)

        def w_at(at_round, *ticks):
            @pl.when(it == at_round)
            def _():
                w_ticks(*ticks)

        @when(it)
        def _():
            begin(it)

        w_at(0, (0, 4), (0, 5), (1, 1))
        w_at(1, (1, 2))

        @when(it - 2)
        def _():
            arrive(it - 2, 2)

        w_at(2, (2, 1), (1, 4))
        w_at(3, (2, 4))

        @when(it - 1)
        def _():
            arrive(it - 1, 1)

        w_at(1, (2, 0), (1, 3))
        w_at(2, (2, 2))
        some_pairs(it - 7, 2)

        @when(it - 6)
        def _():
            ring_end(it - 6)

        some_pairs(it - 6, 0)

        @when(it - 5)
        def _():
            ring_tick(it - 5, 1)

        @when(it - 3)
        def _():
            arrive(it - 3, 4)

        some_pairs(it - 6, 1)

        @when(it - 4)
        def _():
            ring_begin(it - 4)

        @pl.when(it == 3)
        def _():
            w_ticks((2, 5))

            @pl.when(same)
            def _():
                w_copy.wait()

        @when(it - 3)
        def _():
            project(it - 3)

        @when(it - 5)
        def _():
            ring_tick(it - 5, 2)

        @when(it - 2)
        def _():
            arrive(it - 2, 3)

        w_at(2, (1, 5), (2, 3))
        return carry

    lax.fori_loop(0, CHUNKS + 6, round_of, 0)

    last = CHUNKS - 1

    def closing(m, carry):
        pair(m, last)
        finish(m)
        return carry

    lax.fori_loop(0, last, closing, 0)
    pairs(last, last, 2 * last + 1)
    finish(last)

    rim_copy.wait_send()
    for k in range(1, CTX):

        @pl.when(me + k < CTX)
        def _(k=k):
            state_copy(k, me).wait_send()

    @pl.when(crossed)
    def _():
        for i in range(6):
            wy_copy(i).wait_send()
            for step in (1, 2):
                for direction in (0, 1):
                    wx_copy(i, step, direction, True).wait_send()

    def sent(n, carry):
        @pl.when(crossed)
        def _():
            y_copy(n).wait_send()

        for direction in (0, 1):
            for step in (1, 2, 3, 4):
                z_copy(n, step, direction, True).wait_send()
            for step in (1, 2):
                ring_copy(n, step, direction, True).wait_send()
        d_copy(n, True).wait_send()
        core_copy(n, True).wait_send()
        for which in (0, 1):

            @pl.when(jnp.logical_not(jnp.logical_and(same, yhi == which)))
            def _(which=which):
                for copy in home_copies(n, which):
                    copy.wait_send()

        o_copy(n, head_lanes).wait_send()
        return carry

    lax.fori_loop(0, CHUNKS, sent, 0)
    hyena_copy.wait()
    for m in range(CHUNKS):
        o_copy(m, other_lanes).wait_recv()
    att_copy = pltpu.make_async_copy(att, att_hbm, local_sem.at[3])
    att_copy.start()
    att_copy.wait()


def hand_over(a_ref, b_ref, a_out, b_out):
    a_out[...] = a_ref[...]
    b_out[...] = b_ref[...]


def per_device(token_ids, feature_table, short_filter, rates, residues, skip_weight, w_qkv):
    rows = token_ids.shape[0]
    vocab, _, chans = feature_table.shape
    modes = rates.shape[1]
    all_chans, _, width = w_qkv.shape
    f32, bf16 = jnp.float32, jnp.bfloat16
    dma = pltpu.SemaphoreType.DMA
    vmem = pl.BlockSpec(memory_space=pltpu.VMEM)
    hbm = pl.BlockSpec(memory_space=pl.ANY)
    made = pl.pallas_call(
        mixer_kernel,
        out_shape=(
            jax.ShapeDtypeStruct((rows, chans), bf16),
            jax.ShapeDtypeStruct((rows, width), bf16),
        ),
        in_specs=[vmem, hbm, vmem, vmem, vmem, vmem, hbm],
        out_specs=(hbm, hbm),
        scratch_shapes=[
            pltpu.VMEM((3, vocab, chans), bf16),
            pltpu.VMEM((rows, vocab), bf16),
            pltpu.VMEM((3, all_chans, width), bf16),
            pltpu.VMEM((3, 8 + rows, chans), f32),
            pltpu.VMEM((chans // 128, rows, 128), f32),
            pltpu.VMEM((chans // 128, rows, 128), f32),
            pltpu.VMEM((chans // 128, rows, 128), f32),
            pltpu.VMEM((rows // 128, 128), jnp.int32),
            pltpu.VMEM((modes, SEGS, chans), f32),
            pltpu.VMEM((modes, SEGS, chans), f32),
            pltpu.VMEM((modes, SEGS, chans), f32),
            pltpu.VMEM((modes, SEGS, chans), f32),
            pltpu.VMEM((CTX, modes, chans), f32),
            pltpu.VMEM((rows, chans), bf16),
            pltpu.VMEM((rows, all_chans), bf16),
            pltpu.VMEM((CHUNKS, 2, 2, 4, rows // CHUNKS, 2 * HEAD_DIM), bf16),
            pltpu.VMEM((2, rows, HEAD_DIM), bf16),
            pltpu.VMEM((2, rows, 2 * HEAD_DIM), bf16),
            pltpu.VMEM((2, rows, HEAD_DIM), bf16),
            pltpu.VMEM((2, rows, 2 * HEAD_DIM), f32),
            pltpu.VMEM((2, rows, HEAD_DIM), f32),
            pltpu.VMEM((2, rows, HEAD_DIM), bf16),
            pltpu.VMEM((rows, width), bf16),
            dma((4,)),
            dma((2,)),
            dma((CTX - 1,)),
            dma((CTX - 1,)),
            dma((6,)),
            dma((6,)),
            dma((24,)),
            dma((24,)),
            dma((CHUNKS,)),
            dma((CHUNKS,)),
            dma((CHUNKS * 8,)),
            dma((CHUNKS * 8,)),
            dma((CHUNKS,)),
            dma((CHUNKS,)),
            dma((CHUNKS * 4,)),
            dma((CHUNKS * 4,)),
            dma((CHUNKS * 2,)),
            dma((CHUNKS,)),
            dma((CHUNKS,)),
            dma((CHUNKS * 4,)),
            dma((CHUNKS * 4,)),
            dma((CHUNKS,)),
            dma((CHUNKS,)),
        ],
        compiler_params=pltpu.CompilerParams(
            collective_id=0, has_side_effects=True, vmem_limit_bytes=56 * 1024 * 1024
        ),
        name="mixer",
    )(
        token_ids.reshape(rows // 128, 128),
        jnp.transpose(feature_table, (1, 0, 2)),
        short_filter,
        rates.T,
        residues.T,
        skip_weight.reshape(1, chans),
        jnp.transpose(w_qkv, (1, 0, 2)),
    )
    return pl.pallas_call(
        hand_over,
        out_shape=tuple(jax.ShapeDtypeStruct(a.shape, a.dtype) for a in made),
        grid=(2,),
        in_specs=[pl.BlockSpec((rows // 2, a.shape[1]), lambda i: (i, 0)) for a in made],
        out_specs=tuple(pl.BlockSpec((rows // 2, a.shape[1]), lambda i: (i, 0)) for a in made),
        name="hand_over",
    )(*made)


def solution(mesh):
    in_specs = (
        P("ctx"),
        P(None, None, "mp"),
        P(None, None, "mp"),
        P("mp", None),
        P("mp", None),
        P("mp"),
        P(None, None, "mp"),
    )
    out_specs = (P("ctx", "mp"), P("ctx", "mp"))
    return jax.shard_map(
        per_device, mesh=mesh, in_specs=in_specs, out_specs=out_specs, check_vma=False
    )
```

```python
import functools
import math

import jax
import jax.numpy as jnp
from jax import lax
from jax.experimental import pallas as pl
from jax.experimental.pallas import tpu as pltpu
from jax.sharding import PartitionSpec as P

MESH = pl.DeviceIdType.MESH
HEAD_DIM = 128
TAPS = 3
SEGS = 8
NEG_FILL = -1e30
NORM_EPSILON = 1e-06

CTX = 16
MP = 16
PLANE = 8
CHUNKS = 4


def mixer_kernel(
    ids_ref, table_hbm, filt_ref, rates_ref, resid_ref, skip_ref, w_hbm,
    hyena_hbm, att_hbm,
    table, hot, w, feats, gate, lead, mixed, rim, decay, weight, ends, starts, states,
    own, x, kv, qs, kv_out, q_out, q_acc, q_max, o_out, att,
    local_sem, rim_sem, state_send, state_recv,
    wy_send, wy_recv, wx_send, wx_recv,
    y_send, y_recv, z_send, z_recv, d_send, d_recv,
    h_send, h_recv, l_sem, c_send, c_recv, r_send, r_recv, o_send, o_recv,
):
    rows = feats.shape[1] - 8
    chans = feats.shape[2]
    modes = decay.shape[0]
    steps = rows // SEGS
    part = rows // CHUNKS
    half = part // 2
    all_chans = x.shape[1]
    total_len = CTX * rows
    span = CTX * part

    me = lax.axis_index("ctx")
    mp = lax.axis_index("mp")
    core = me % 2
    xpos = (me // 2) % 4
    yhi = me // 8
    zpos = mp % PLANE
    ylo = mp // PLANE
    sibling = me + 1 - 2 * core
    opposite = (me + 8) % CTX
    x_right = yhi * 8 + 2 * ((xpos + 1) % 4) + core
    x_left = yhi * 8 + 2 * ((xpos + 3) % 4) + core
    z_right = ylo * PLANE + (zpos + 1) % PLANE
    z_left = ylo * PLANE + (zpos + PLANE - 1) % PLANE
    y_other = (1 - ylo) * PLANE + zpos
    same = ylo == core
    crossed = ylo != core

    def remote(src, dst, send, recv, **target):
        return pltpu.make_async_remote_copy(
            src_ref=src, dst_ref=dst, send_sem=send, recv_sem=recv,
            device_id=target, device_id_type=MESH,
        )

    table_copy = pltpu.make_async_copy(table_hbm, table, local_sem.at[0])
    table_copy.start()
    w_copy = pltpu.make_async_copy(w_hbm, w, local_sem.at[1])

    @pl.when(same)
    def _():
        w_copy.start()

    barrier = pltpu.get_barrier_semaphore()
    for k in range(1, CTX):
        pl.semaphore_signal(
            barrier, inc=1, device_id={"ctx": (me + k) % CTX}, device_id_type=MESH
        )
    for other in (z_right, z_left):
        pl.semaphore_signal(barrier, inc=1, device_id={"mp": other}, device_id_type=MESH)
    for other in (sibling, (sibling + 8) % CTX):
        pl.semaphore_signal(
            barrier, inc=1, device_id={"ctx": other, "mp": y_other}, device_id_type=MESH
        )
    vocab = table.shape[1]
    place = lax.broadcasted_iota(jnp.int32, (128, 128), 1)

    def one_hot(ids_row):
        ids = jnp.transpose(jnp.broadcast_to(ids_row, (128, 128)))
        hits = [(ids == place + at).astype(jnp.float32) for at in range(0, vocab, 128)]
        return jnp.concatenate(hits, axis=1).astype(jnp.bfloat16)

    for r in range(rows // 128):
        hot[r * 128 : (r + 1) * 128, :] = one_hot(ids_ref[r : r + 1, :])
    table_copy.wait()
    for j in range(3):
        feats[j, 8:, :] = jnp.dot(hot[...], table[j], preferred_element_type=jnp.float32)

    pl.semaphore_wait(barrier, CTX - 1 + 4)

    rim_copy = remote(ids_ref, rim, rim_sem.at[0], rim_sem.at[1], ctx=(me + 1) % CTX)
    rim_copy.start()

    quarter = all_chans // 4
    piece = quarter // 2

    def w_rows(i, place, shift=0, count=piece):
        at = (place % 4) * quarter + (i % 2) * piece + shift
        return pl.ds(pl.multiple_of(at, 16), count)

    def wy_copy(i):
        at = w_rows(i, xpos)
        return remote(
            w_hbm.at[i // 2, at, :], w.at[i // 2, at, :], wy_send.at[i], wy_recv.at[i],
            ctx=sibling if i % 2 == 0 else (sibling + 8) % CTX, mp=y_other,
        )

    def wx_copy(i, step, direction, outgoing):
        sign = 3 if direction == 0 else 1
        away = sign * (step - 1 if outgoing else step)
        cut = (0, piece) if step == 1 else (direction * piece // 2, piece // 2)
        ref = w.at[i // 2, w_rows(i, xpos + away, *cut), :]
        k = (i * 2 + step - 1) * 2 + direction
        return remote(
            ref, ref, wx_send.at[k], wx_recv.at[k], ctx=x_right if direction == 0 else x_left
        )

    def w_ticks(*ticks):
        @pl.when(crossed)
        def _():
            for step, i in ticks:
                if step == 0:
                    wy_copy(i).wait_recv()
                for direction in (0, 1):
                    if step > 0:
                        wx_copy(i, step, direction, False).wait_recv()
                    if step < 2:
                        wx_copy(i, step + 1, direction, True).start()

    @pl.when(crossed)
    def _():
        for i in range(6):
            wy_copy(i).start()

    damping = rates_ref[...] / total_len
    twice = 2.0 * damping
    small = twice * (
        1.0
        - twice
        * (
            0.5
            - twice
            * (1.0 / 6 - twice * (1.0 / 24 - twice * (1.0 / 120 - twice * (1.0 / 720))))
        )
    )
    grown = jnp.where(twice < 0.1, small, 1.0 - jnp.exp(-twice))
    mode_weight = resid_ref[...] * jnp.sqrt(grown)
    one_step = jnp.exp(-damping)
    for r in range(modes):
        decay[r] = jnp.broadcast_to(one_step[r : r + 1, :], (SEGS, chans))
        weight[r] = jnp.broadcast_to(mode_weight[r : r + 1, :], (SEGS, chans))

    def smooth(j, at, count):
        total = filt_ref[0, j : j + 1, :] * feats[j, 8 + at : 8 + at + count, :]
        for tap in range(1, TAPS):
            total = total + filt_ref[tap, j : j + 1, :] * feats[
                j, 8 + at - tap : 8 + at - tap + count, :
            ]
        return total

    groups = [(g, slice(g * 128, (g + 1) * 128)) for g in range(chans // 128)]
    def smooth_all(at):
        gated = smooth(1, at, 96) * smooth(2, at, 96)
        led = smooth(0, at, 96)
        for g, lanes in groups:
            gate[g, at : at + 96, :] = gated[:, lanes]
            lead[g, at : at + 96, :] = led[:, lanes]

    for at in range(96, rows, 96):
        smooth_all(at)
    rim_copy.wait_recv()
    before_hot = one_hot(rim[rows // 128 - 1 : rows // 128, :])[112:128, :]
    for j in range(3):
        before = jnp.dot(before_hot, table[j], preferred_element_type=jnp.float32)[8:16, :]
        feats[j, 0:8, :] = jnp.where(me > 0, before, 0.0)
    smooth_all(0)

    for g, lanes in groups:
        fade = decay[:, :, lanes]

        def ended(i, state, g=g, fade=fade):
            row = gate[g, pl.ds(i, SEGS, stride=steps), :]
            return fade * state + row[None]

        ends[:, :, lanes] = lax.fori_loop(
            0, steps, ended, jnp.zeros((modes, SEGS, 128), jnp.float32), unroll=4
        )
    segment_fade = jnp.exp(-damping * steps)
    running = jnp.zeros((modes, chans), jnp.float32)
    for j in range(SEGS):
        starts[:, j, :] = running
        running = segment_fade * running + ends[:, j, :]
    states[me] = running

    def state_copy(k, owner):
        ref = states.at[owner]
        return remote(
            ref, ref, state_send.at[k - 1], state_recv.at[k - 1], ctx=(me + k) % CTX
        )

    for k in range(1, CTX):

        @pl.when(me + k < CTX)
        def _(k=k):
            state_copy(k, me).start()

    w_ticks((0, 0), (0, 1))
    q_acc[...] = jnp.zeros_like(q_acc)
    q_max[...] = jnp.full_like(q_max, NEG_FILL)
    for k in range(1, CTX):

        @pl.when(me >= k)
        def _(k=k):
            state_copy(k, (me + CTX - k) % CTX).wait_recv()

    def gathered(k, total):
        gap = (me - 1 - k).astype(jnp.float32) * rows
        return total + jnp.exp(-damping * gap) * states[k]

    incoming = lax.fori_loop(0, me, gathered, jnp.zeros((modes, chans), jnp.float32))
    for j in range(SEGS):
        starts[:, j, :] += jnp.exp(-damping * (steps * j)) * incoming
    w_ticks((0, 2), (0, 3))

    for g, lanes in groups:
        fade = decay[:, :, lanes]
        skip = skip_ref[:, lanes]

        def stepped(i, state, g=g, lanes=lanes, fade=fade, skip=skip):
            at = pl.ds(i, SEGS, stride=steps)
            row = gate[g, at, :]
            state = fade * state + row[None]
            conv = jnp.sum(weight[:, :, lanes] * state, axis=0)
            mixed[g, at, :] = lead[g, at, :] * (conv + skip * row)
            return state

        lax.fori_loop(0, steps, stepped, starts[:, :, lanes], unroll=2)

    def columns(plane, z_at):
        return pl.ds(pl.multiple_of((plane * PLANE + z_at) * chans, chans), chans)

    made_out = jnp.concatenate([mixed[g] for g, _ in groups], axis=1).astype(jnp.bfloat16)
    own[...] = made_out

    @pl.when(same)
    def _():
        x[:, columns(ylo, zpos)] = own[...]

    def rows_of(n, shift=0, count=part):
        return pl.ds(pl.multiple_of(n * part + shift, 16), count)

    def y_copy(n):
        return remote(
            own.at[rows_of(n), :], x.at[rows_of(n), columns(ylo, zpos)],
            y_send.at[n], y_recv.at[n], ctx=sibling, mp=y_other,
        )

    @pl.when(crossed)
    def _():
        for n in range(CHUNKS):
            y_copy(n).start()

    hyena_copy = pltpu.make_async_copy(own, hyena_hbm, local_sem.at[2])
    hyena_copy.start()
    w_ticks((1, 0))

    def z_part(n, step, direction, plane, outgoing):
        away = step - 1 if outgoing else step
        origin = (zpos + PLANE - away) % PLANE if direction == 0 else (zpos + away) % PLANE
        count, shift = (half, direction * half) if step == 4 else (part, 0)
        return x.at[rows_of(n, shift, count), columns(plane, origin)]

    def z_copy(n, step, direction, outgoing):
        ref = z_part(n, step, direction, core, outgoing)
        k = (n * 4 + step - 1) * 2 + direction
        return remote(
            ref, ref, z_send.at[k], z_recv.at[k], mp=z_right if direction == 0 else z_left
        )

    def d_copy(n, outgoing):
        plane = core if outgoing else 1 - core
        width = PLANE * chans
        ref = x.at[rows_of(n), pl.ds(pl.multiple_of(plane * width, width), width)]
        return remote(ref, ref, d_send.at[n], d_recv.at[n], ctx=sibling)

    def begin(n):
        @pl.when(crossed)
        def _():
            y_copy(n).wait_recv()

        for direction in (0, 1):
            z_copy(n, 1, direction, True).start()

    def arrive(n, step):
        for direction in (0, 1):
            z_copy(n, step, direction, False).wait_recv()
            if step < 4:
                z_copy(n, step + 1, direction, True).start()
        if step == 4:
            d_copy(n, True).start()

    def block_of(which, place, at_core):
        return which * 8 + 2 * place + at_core

    def kv_home(which, at_core, n):
        return kv.at[n, which, at_core, xpos]

    def home_copies(n, head):
        at = rows_of(n)
        k = (n * 2 + head) * 2
        r = (n * 2 + yhi) * 2
        target = {"ctx": block_of(head, xpos, ylo), "mp": core * PLANE + zpos}
        return (
            remote(
                kv_out.at[head, at, :], kv_home(yhi, ylo, n),
                h_send.at[k], h_recv.at[r], **target,
            ),
            remote(
                q_out.at[head, at, :], qs.at[yhi, at, :],
                h_send.at[k + 1], h_recv.at[r + 1], **target,
            ),
        )

    def local_copies(n, head):
        at = rows_of(n)
        return (
            pltpu.make_async_copy(
                kv_out.at[head, at, :], kv_home(yhi, ylo, n), l_sem.at[n * 2]
            ),
            pltpu.make_async_copy(
                q_out.at[head, at, :], qs.at[yhi, at, :], l_sem.at[n * 2 + 1]
            ),
        )

    def home_waits(n, which):
        at = rows_of(n)
        k = (n * 2 + which) * 2
        at_home = jnp.logical_and(same, yhi == which)

        @pl.when(at_home)
        def _():
            for copy in local_copies(n, which):
                copy.wait()

        @pl.when(jnp.logical_not(at_home))
        def _():
            target = {"ctx": block_of(which, xpos, ylo), "mp": core * PLANE + zpos}
            remote(
                kv_out.at[0, at, :], kv_home(which, core, n),
                h_send.at[k], h_recv.at[k], **target,
            ).wait_recv()
            remote(
                q_out.at[0, at, :], qs.at[which, at, :], h_send.at[k + 1], h_recv.at[k + 1],
                **target,
            ).wait_recv()

    def ring_copy(n, step, direction, outgoing):
        sign = 3 if direction == 0 else 1
        away = step - 1 if outgoing else step
        at = slice(0, part) if step == 1 else slice(direction * half, direction * half + half)
        ref = kv.at[n, :, core, (xpos + sign * away) % 4, at, :]
        k = (n * 2 + step - 1) * 2 + direction
        return remote(
            ref, ref, r_send.at[k], r_recv.at[k], ctx=x_right if direction == 0 else x_left
        )

    def core_copy(n, outgoing):
        ref = kv.at[n, :, core if outgoing else 1 - core]
        return remote(ref, ref, c_send.at[n], c_recv.at[n], ctx=sibling)

    def ring_begin(n):
        for which in (0, 1):
            home_waits(n, which)
        for direction in (0, 1):
            ring_copy(n, 1, direction, True).start()

    def ring_tick(n, step):
        for direction in (0, 1):
            ring_copy(n, step, direction, False).wait_recv()
            if step == 1:
                ring_copy(n, 2, direction, True).start()
        if step == 2:
            core_copy(n, True).start()

    def ring_end(n):
        core_copy(n, False).wait_recv()

    def project(n):
        d_copy(n, False).wait_recv()
        at = rows_of(n)
        wide = x[at, :].astype(jnp.float32)
        squares = jnp.sum(wide * wide, axis=1, keepdims=True)
        norm = lax.rsqrt(squares / all_chans + NORM_EPSILON)
        for j in range(3):
            scale = norm * (math.log2(math.e) / math.sqrt(HEAD_DIM)) if j == 0 else norm
            made = jnp.dot(x[at, :], w[j], preferred_element_type=jnp.float32) * scale
            made = made.astype(jnp.bfloat16)
            for head in (0, 1):
                piece = made[:, head * HEAD_DIM : (head + 1) * HEAD_DIM]
                if j == 0:
                    q_out[head, at, :] = piece
                else:
                    kv_out[head, at, (j - 1) * HEAD_DIM : j * HEAD_DIM] = piece
        for head in (0, 1):
            stays = jnp.logical_and(same, yhi == head)

            @pl.when(stays)
            def _(head=head):
                for copy in local_copies(n, head):
                    copy.start()

            @pl.when(jnp.logical_not(stays))
            def _(head=head):
                for copy in home_copies(n, head):
                    copy.start()

    ones = jnp.ones((span // 2, HEAD_DIM), jnp.bfloat16)

    def scores_of(queries, block):
        return lax.dot_general(
            queries, block[:, :HEAD_DIM], (((1,), (1,)), ((), ())),
            preferred_element_type=jnp.float32,
        )

    def masked(scores, bounds):
        width = scores.shape[1] // 2
        col = lax.broadcasted_iota(jnp.int32, (part, width), 1)
        return jnp.concatenate(
            [
                jnp.where(col < bound, scores[:, i * width : (i + 1) * width], NEG_FILL)
                for i, bound in enumerate(bounds)
            ],
            axis=1,
        )

    def pair(q_chunk, k_chunk):
        at = rows_of(q_chunk)
        row = lax.broadcasted_iota(jnp.int32, (part, 1), 0) + 1
        extra = jnp.where(k_chunk < q_chunk, part, jnp.where(k_chunk == q_chunk, row, 0))
        bounds = [
            xpos * part + jnp.where(core == 0, extra, part),
            xpos * part + jnp.where(core == 0, 0, extra),
        ]
        low = kv[k_chunk, 0].reshape(span // 2, 2 * HEAD_DIM)
        high = kv[k_chunk, 1].reshape(span // 2, 2 * HEAD_DIM)
        for which in (1, 0):
            queries = qs[which, at, :]
            if which == 1:
                blocks = [low, high]
                scores = [scores_of(queries, low), masked(scores_of(queries, high), bounds)]
            else:
                blocks = [low]
                scores = [masked(scores_of(queries, low), bounds)]
            old = q_max[which, at, :]
            new = old
            for s in scores:
                new = jnp.maximum(new, jnp.max(s, axis=1, keepdims=True))
            wide = jnp.concatenate([new] * (span // 256), axis=1)
            shrink = jnp.exp2(old - new)
            total = q_acc[which, at, :] * jnp.concatenate([shrink, shrink], axis=1)
            for s, block in zip(scores, blocks):
                weights = jnp.exp2(s - wide).astype(jnp.bfloat16)
                values = jnp.concatenate([block[:, HEAD_DIM:], ones], axis=1)
                total = total + jnp.dot(weights, values, preferred_element_type=jnp.float32)
            q_acc[which, at, :] = total
            q_max[which, at, :] = new

    def early_pairs(n, first, last):
        def one(i, carry):
            pair(n, i)
            return carry

        lax.fori_loop(first, last, one, 0)

    def late_pairs(n, first, last):
        def one(i, carry):
            pair(i, n)
            return carry

        lax.fori_loop(first, last, one, 0)

    head_lanes = pl.ds(pl.multiple_of(yhi * HEAD_DIM, HEAD_DIM), HEAD_DIM)
    other_lanes = pl.ds(pl.multiple_of((1 - yhi) * HEAD_DIM, HEAD_DIM), HEAD_DIM)

    def o_copy(m, lanes):
        at = rows_of(m)
        return remote(
            o_out.at[1 - yhi, at, :], att.at[at, lanes], o_send.at[m], o_recv.at[m], ctx=opposite
        )

    def finish(m):
        at = rows_of(m)
        for which in (0, 1):
            done = q_acc[which, at, :HEAD_DIM] / q_acc[which, at, HEAD_DIM:]
            o_out[which, at, :] = done.astype(jnp.bfloat16)
        o_copy(m, head_lanes).start()
        att[at, head_lanes] = o_out[yhi, at, :]

    def round_of(it, carry):
        def when(n):
            return pl.when(jnp.logical_and(n >= 0, n < CHUNKS))

        def some_early(n, piece):
            @when(n)
            def _():
                early_pairs(n, n * piece // 2, n * (piece + 1) // 2)

        def some_late(n, piece):
            @pl.when(jnp.logical_and(n >= 0, n < CHUNKS - 1))
            def _():
                count = n + 1
                late_pairs(n, count * piece // 3, count * (piece + 1) // 3)

        def w_at(at_round, *ticks):
            @pl.when(it == at_round)
            def _():
                w_ticks(*ticks)

        @when(it)
        def _():
            begin(it)

        w_at(0, (0, 4), (0, 5), (1, 1))
        w_at(1, (1, 2))

        @when(it - 2)
        def _():
            arrive(it - 2, 2)

        w_at(2, (2, 1), (1, 4))
        w_at(3, (2, 4))

        @when(it - 1)
        def _():
            arrive(it - 1, 1)

        w_at(1, (2, 0), (1, 3))
        w_at(2, (2, 2))
        some_late(it - 7, 2)

        @when(it - 6)
        def _():
            ring_end(it - 6)

        some_late(it - 6, 0)

        @when(it - 5)
        def _():
            ring_tick(it - 5, 1)

        @when(it - 3)
        def _():
            arrive(it - 3, 4)

        some_late(it - 6, 1)

        @when(it - 4)
        def _():
            ring_begin(it - 4)

        some_early(it - 4, 0)

        @pl.when(it == 3)
        def _():
            w_ticks((2, 5))

            @pl.when(same)
            def _():
                w_copy.wait()

        @when(it - 3)
        def _():
            project(it - 3)

        some_early(it - 5, 1)

        @when(it - 5)
        def _():
            ring_tick(it - 5, 2)

        @when(it - 2)
        def _():
            arrive(it - 2, 3)

        w_at(2, (1, 5), (2, 3))
        return carry

    lax.fori_loop(0, CHUNKS + 6, round_of, 0)

    last = CHUNKS - 1

    def closing(m, carry):
        pair(m, last)
        finish(m)
        return carry

    lax.fori_loop(0, CHUNKS, closing, 0)

    rim_copy.wait_send()
    for k in range(1, CTX):

        @pl.when(me + k < CTX)
        def _(k=k):
            state_copy(k, me).wait_send()

    @pl.when(crossed)
    def _():
        for i in range(6):
            wy_copy(i).wait_send()
            for step in (1, 2):
                for direction in (0, 1):
                    wx_copy(i, step, direction, True).wait_send()

    def sent(n, carry):
        @pl.when(crossed)
        def _():
            y_copy(n).wait_send()

        for direction in (0, 1):
            for step in (1, 2, 3, 4):
                z_copy(n, step, direction, True).wait_send()
            for step in (1, 2):
                ring_copy(n, step, direction, True).wait_send()
        d_copy(n, True).wait_send()
        core_copy(n, True).wait_send()
        for which in (0, 1):

            @pl.when(jnp.logical_not(jnp.logical_and(same, yhi == which)))
            def _(which=which):
                for copy in home_copies(n, which):
                    copy.wait_send()

        o_copy(n, head_lanes).wait_send()
        return carry

    lax.fori_loop(0, CHUNKS, sent, 0)
    hyena_copy.wait()
    for m in range(CHUNKS):
        o_copy(m, other_lanes).wait_recv()
    att_copy = pltpu.make_async_copy(att, att_hbm, local_sem.at[3])
    att_copy.start()
    att_copy.wait()


def hand_over(a_ref, b_ref, a_out, b_out):
    a_out[...] = a_ref[...]
    b_out[...] = b_ref[...]


def per_device(token_ids, feature_table, short_filter, rates, residues, skip_weight, w_qkv):
    rows = token_ids.shape[0]
    vocab, _, chans = feature_table.shape
    modes = rates.shape[1]
    all_chans, _, width = w_qkv.shape
    f32, bf16 = jnp.float32, jnp.bfloat16
    dma = pltpu.SemaphoreType.DMA
    vmem = pl.BlockSpec(memory_space=pltpu.VMEM)
    hbm = pl.BlockSpec(memory_space=pl.ANY)
    made = pl.pallas_call(
        mixer_kernel,
        out_shape=(
            jax.ShapeDtypeStruct((rows, chans), bf16),
            jax.ShapeDtypeStruct((rows, width), bf16),
        ),
        in_specs=[vmem, hbm, vmem, vmem, vmem, vmem, hbm],
        out_specs=(hbm, hbm),
        scratch_shapes=[
            pltpu.VMEM((3, vocab, chans), bf16),
            pltpu.VMEM((rows, vocab), bf16),
            pltpu.VMEM((3, all_chans, width), bf16),
            pltpu.VMEM((3, 8 + rows, chans), f32),
            pltpu.VMEM((chans // 128, rows, 128), f32),
            pltpu.VMEM((chans // 128, rows, 128), f32),
            pltpu.VMEM((chans // 128, rows, 128), f32),
            pltpu.VMEM((rows // 128, 128), jnp.int32),
            pltpu.VMEM((modes, SEGS, chans), f32),
            pltpu.VMEM((modes, SEGS, chans), f32),
            pltpu.VMEM((modes, SEGS, chans), f32),
            pltpu.VMEM((modes, SEGS, chans), f32),
            pltpu.VMEM((CTX, modes, chans), f32),
            pltpu.VMEM((rows, chans), bf16),
            pltpu.VMEM((rows, all_chans), bf16),
            pltpu.VMEM((CHUNKS, 2, 2, 4, rows // CHUNKS, 2 * HEAD_DIM), bf16),
            pltpu.VMEM((2, rows, HEAD_DIM), bf16),
            pltpu.VMEM((2, rows, 2 * HEAD_DIM), bf16),
            pltpu.VMEM((2, rows, HEAD_DIM), bf16),
            pltpu.VMEM((2, rows, 2 * HEAD_DIM), f32),
            pltpu.VMEM((2, rows, HEAD_DIM), f32),
            pltpu.VMEM((2, rows, HEAD_DIM), bf16),
            pltpu.VMEM((rows, width), bf16),
            dma((4,)),
            dma((2,)),
            dma((CTX - 1,)),
            dma((CTX - 1,)),
            dma((6,)),
            dma((6,)),
            dma((24,)),
            dma((24,)),
            dma((CHUNKS,)),
            dma((CHUNKS,)),
            dma((CHUNKS * 8,)),
            dma((CHUNKS * 8,)),
            dma((CHUNKS,)),
            dma((CHUNKS,)),
            dma((CHUNKS * 4,)),
            dma((CHUNKS * 4,)),
            dma((CHUNKS * 2,)),
            dma((CHUNKS,)),
            dma((CHUNKS,)),
            dma((CHUNKS * 4,)),
            dma((CHUNKS * 4,)),
            dma((CHUNKS,)),
            dma((CHUNKS,)),
        ],
        compiler_params=pltpu.CompilerParams(
            collective_id=0, has_side_effects=True, vmem_limit_bytes=56 * 1024 * 1024
        ),
        name="mixer",
    )(
        token_ids.reshape(rows // 128, 128),
        jnp.transpose(feature_table, (1, 0, 2)),
        short_filter,
        rates.T,
        residues.T,
        skip_weight.reshape(1, chans),
        jnp.transpose(w_qkv, (1, 0, 2)),
    )
    return pl.pallas_call(
        hand_over,
        out_shape=tuple(jax.ShapeDtypeStruct(a.shape, a.dtype) for a in made),
        grid=(2,),
        in_specs=[pl.BlockSpec((rows // 2, a.shape[1]), lambda i: (i, 0)) for a in made],
        out_specs=tuple(pl.BlockSpec((rows // 2, a.shape[1]), lambda i: (i, 0)) for a in made),
        name="hand_over",
    )(*made)


def solution(mesh):
    in_specs = (
        P("ctx"),
        P(None, None, "mp"),
        P(None, None, "mp"),
        P("mp", None),
        P("mp", None),
        P("mp"),
        P(None, None, "mp"),
    )
    out_specs = (P("ctx", "mp"), P("ctx", "mp"))
    return jax.shard_map(
        per_device, mesh=mesh, in_specs=in_specs, out_specs=out_specs, check_vma=False
    )
```

```python
import functools
import math

import jax
import jax.numpy as jnp
from jax import lax
from jax.experimental import pallas as pl
from jax.experimental.pallas import tpu as pltpu
from jax.sharding import PartitionSpec as P

MESH = pl.DeviceIdType.MESH
HEAD_DIM = 128
TAPS = 3
SEGS = 8
NEG_FILL = -1e30
NORM_EPSILON = 1e-06

CTX = 16
MP = 16
PLANE = 8
CHUNKS = 4


def mixer_kernel(
    ids_ref, table_hbm, filt_ref, rates_ref, resid_ref, skip_ref, w_hbm,
    hyena_hbm, att_hbm,
    table, hot, w, feats, gate, lead, mixed, rim, decay, weight, ends, starts, states,
    own, x, kv, qs, kv_out, q_out, q_acc, q_max, o_out, att,
    local_sem, rim_sem, state_send, state_recv,
    wy_send, wy_recv, wx_send, wx_recv,
    y_send, y_recv, z_send, z_recv, d_send, d_recv,
    h_send, h_recv, l_sem, c_send, c_recv, r_send, r_recv, o_send, o_recv,
):
    rows = feats.shape[1] - 8
    chans = feats.shape[2]
    modes = decay.shape[0]
    steps = rows // SEGS
    part = rows // CHUNKS
    half = part // 2
    all_chans = x.shape[1]
    total_len = CTX * rows
    span = CTX * part

    me = lax.axis_index("ctx")
    mp = lax.axis_index("mp")
    core = me % 2
    xpos = (me // 2) % 4
    yhi = me // 8
    zpos = mp % PLANE
    ylo = mp // PLANE
    sibling = me + 1 - 2 * core
    opposite = (me + 8) % CTX
    x_right = yhi * 8 + 2 * ((xpos + 1) % 4) + core
    x_left = yhi * 8 + 2 * ((xpos + 3) % 4) + core
    z_right = ylo * PLANE + (zpos + 1) % PLANE
    z_left = ylo * PLANE + (zpos + PLANE - 1) % PLANE
    y_other = (1 - ylo) * PLANE + zpos
    same = ylo == core
    crossed = ylo != core

    def remote(src, dst, send, recv, **target):
        return pltpu.make_async_remote_copy(
            src_ref=src, dst_ref=dst, send_sem=send, recv_sem=recv,
            device_id=target, device_id_type=MESH,
        )

    table_copy = pltpu.make_async_copy(table_hbm, table, local_sem.at[0])
    table_copy.start()
    w_copy = pltpu.make_async_copy(w_hbm, w, local_sem.at[1])

    @pl.when(same)
    def _():
        w_copy.start()

    barrier = pltpu.get_barrier_semaphore()
    for k in range(1, CTX):
        pl.semaphore_signal(
            barrier, inc=1, device_id={"ctx": (me + k) % CTX}, device_id_type=MESH
        )
    for other in (z_right, z_left):
        pl.semaphore_signal(barrier, inc=1, device_id={"mp": other}, device_id_type=MESH)
    for other in (sibling, (sibling + 8) % CTX):
        pl.semaphore_signal(
            barrier, inc=1, device_id={"ctx": other, "mp": y_other}, device_id_type=MESH
        )
    vocab = table.shape[1]
    place = lax.broadcasted_iota(jnp.int32, (128, 128), 1)

    def one_hot(ids_row):
        ids = jnp.transpose(jnp.broadcast_to(ids_row, (128, 128)))
        hits = [(ids == place + at).astype(jnp.float32) for at in range(0, vocab, 128)]
        return jnp.concatenate(hits, axis=1).astype(jnp.bfloat16)

    for r in range(rows // 128):
        hot[r * 128 : (r + 1) * 128, :] = one_hot(ids_ref[r : r + 1, :])
    table_copy.wait()
    for j in range(3):
        feats[j, 8:, :] = jnp.dot(hot[...], table[j], preferred_element_type=jnp.float32)

    pl.semaphore_wait(barrier, CTX - 1 + 4)

    rim_copy = remote(ids_ref, rim, rim_sem.at[0], rim_sem.at[1], ctx=(me + 1) % CTX)
    rim_copy.start()

    quarter = all_chans // 4
    piece = quarter // 2

    def w_rows(i, place, shift=0, count=piece):
        at = (place % 4) * quarter + (i % 2) * piece + shift
        return pl.ds(pl.multiple_of(at, 16), count)

    def wy_copy(i):
        at = w_rows(i, xpos)
        return remote(
            w_hbm.at[i // 2, at, :], w.at[i // 2, at, :], wy_send.at[i], wy_recv.at[i],
            ctx=sibling if i % 2 == 0 else (sibling + 8) % CTX, mp=y_other,
        )

    def wx_copy(i, step, direction, outgoing):
        sign = 3 if direction == 0 else 1
        away = sign * (step - 1 if outgoing else step)
        cut = (0, piece) if step == 1 else (direction * piece // 2, piece // 2)
        ref = w.at[i // 2, w_rows(i, xpos + away, *cut), :]
        k = (i * 2 + step - 1) * 2 + direction
        return remote(
            ref, ref, wx_send.at[k], wx_recv.at[k], ctx=x_right if direction == 0 else x_left
        )

    def w_ticks(*ticks):
        @pl.when(crossed)
        def _():
            for step, i in ticks:
                if step == 0:
                    wy_copy(i).wait_recv()
                for direction in (0, 1):
                    if step > 0:
                        wx_copy(i, step, direction, False).wait_recv()
                    if step < 2:
                        wx_copy(i, step + 1, direction, True).start()

    @pl.when(crossed)
    def _():
        for i in range(6):
            wy_copy(i).start()

    damping = rates_ref[...] / total_len
    twice = 2.0 * damping
    small = twice * (
        1.0
        - twice
        * (
            0.5
            - twice
            * (1.0 / 6 - twice * (1.0 / 24 - twice * (1.0 / 120 - twice * (1.0 / 720))))
        )
    )
    grown = jnp.where(twice < 0.1, small, 1.0 - jnp.exp(-twice))
    mode_weight = resid_ref[...] * jnp.sqrt(grown)
    one_step = jnp.exp(-damping)
    for r in range(modes):
        decay[r] = jnp.broadcast_to(one_step[r : r + 1, :], (SEGS, chans))
        weight[r] = jnp.broadcast_to(mode_weight[r : r + 1, :], (SEGS, chans))

    def smooth(j, at, count):
        total = filt_ref[0, j : j + 1, :] * feats[j, 8 + at : 8 + at + count, :]
        for tap in range(1, TAPS):
            total = total + filt_ref[tap, j : j + 1, :] * feats[
                j, 8 + at - tap : 8 + at - tap + count, :
            ]
        return total

    groups = [(g, slice(g * 128, (g + 1) * 128)) for g in range(chans // 128)]
    def smooth_all(at):
        gated = smooth(1, at, 96) * smooth(2, at, 96)
        led = smooth(0, at, 96)
        for g, lanes in groups:
            gate[g, at : at + 96, :] = gated[:, lanes]
            lead[g, at : at + 96, :] = led[:, lanes]

    for at in range(96, rows, 96):
        smooth_all(at)
    rim_copy.wait_recv()
    before_hot = one_hot(rim[rows // 128 - 1 : rows // 128, :])[112:128, :]
    for j in range(3):
        before = jnp.dot(before_hot, table[j], preferred_element_type=jnp.float32)[8:16, :]
        feats[j, 0:8, :] = jnp.where(me > 0, before, 0.0)
    smooth_all(0)

    for g, lanes in groups:
        fade = decay[:, :, lanes]

        def ended(i, state, g=g, fade=fade):
            row = gate[g, pl.ds(i, SEGS, stride=steps), :]
            return fade * state + row[None]

        ends[:, :, lanes] = lax.fori_loop(
            0, steps, ended, jnp.zeros((modes, SEGS, 128), jnp.float32), unroll=4
        )
    segment_fade = jnp.exp(-damping * steps)
    running = jnp.zeros((modes, chans), jnp.float32)
    for j in range(SEGS):
        starts[:, j, :] = running
        running = segment_fade * running + ends[:, j, :]
    states[me] = running

    def state_copy(k, owner):
        ref = states.at[owner]
        return remote(
            ref, ref, state_send.at[k - 1], state_recv.at[k - 1], ctx=(me + k) % CTX
        )

    for k in range(1, CTX):

        @pl.when(me + k < CTX)
        def _(k=k):
            state_copy(k, me).start()

    w_ticks((0, 0), (0, 1))
    q_acc[...] = jnp.zeros_like(q_acc)
    q_max[...] = jnp.full_like(q_max, NEG_FILL)
    for k in range(1, CTX):

        @pl.when(me >= k)
        def _(k=k):
            state_copy(k, (me + CTX - k) % CTX).wait_recv()

    def gathered(k, total):
        gap = (me - 1 - k).astype(jnp.float32) * rows
        return total + jnp.exp(-damping * gap) * states[k]

    incoming = lax.fori_loop(0, me, gathered, jnp.zeros((modes, chans), jnp.float32))
    for j in range(SEGS):
        starts[:, j, :] += jnp.exp(-damping * (steps * j)) * incoming
    w_ticks((0, 2), (0, 3))

    for g, lanes in groups:
        fade = decay[:, :, lanes]
        skip = skip_ref[:, lanes]

        def stepped(i, state, g=g, lanes=lanes, fade=fade, skip=skip):
            at = pl.ds(i, SEGS, stride=steps)
            row = gate[g, at, :]
            state = fade * state + row[None]
            conv = jnp.sum(weight[:, :, lanes] * state, axis=0)
            mixed[g, at, :] = lead[g, at, :] * (conv + skip * row)
            return state

        lax.fori_loop(0, steps, stepped, starts[:, :, lanes], unroll=2)

    def columns(plane, z_at):
        return pl.ds(pl.multiple_of((plane * PLANE + z_at) * chans, chans), chans)

    made_out = jnp.concatenate([mixed[g] for g, _ in groups], axis=1).astype(jnp.bfloat16)
    own[...] = made_out

    @pl.when(same)
    def _():
        x[:, columns(ylo, zpos)] = own[...]

    def rows_of(n, shift=0, count=part):
        return pl.ds(pl.multiple_of(n * part + shift, 16), count)

    def y_copy(n):
        return remote(
            own.at[rows_of(n), :], x.at[rows_of(n), columns(ylo, zpos)],
            y_send.at[n], y_recv.at[n], ctx=sibling, mp=y_other,
        )

    @pl.when(crossed)
    def _():
        for n in range(CHUNKS):
            y_copy(n).start()

    hyena_copy = pltpu.make_async_copy(own, hyena_hbm, local_sem.at[2])
    hyena_copy.start()
    w_ticks((1, 0))

    def z_part(n, step, direction, plane, outgoing):
        away = step - 1 if outgoing else step
        origin = (zpos + PLANE - away) % PLANE if direction == 0 else (zpos + away) % PLANE
        count, shift = (half, direction * half) if step == 4 else (part, 0)
        return x.at[rows_of(n, shift, count), columns(plane, origin)]

    def z_copy(n, step, direction, outgoing):
        ref = z_part(n, step, direction, core, outgoing)
        k = (n * 4 + step - 1) * 2 + direction
        return remote(
            ref, ref, z_send.at[k], z_recv.at[k], mp=z_right if direction == 0 else z_left
        )

    def d_copy(n, outgoing):
        plane = core if outgoing else 1 - core
        width = PLANE * chans
        ref = x.at[rows_of(n), pl.ds(pl.multiple_of(plane * width, width), width)]
        return remote(ref, ref, d_send.at[n], d_recv.at[n], ctx=sibling)

    def begin(n):
        @pl.when(crossed)
        def _():
            y_copy(n).wait_recv()

        for direction in (0, 1):
            z_copy(n, 1, direction, True).start()

    def arrive(n, step):
        for direction in (0, 1):
            z_copy(n, step, direction, False).wait_recv()
            if step < 4:
                z_copy(n, step + 1, direction, True).start()
        if step == 4:
            d_copy(n, True).start()

    def block_of(which, place, at_core):
        return which * 8 + 2 * place + at_core

    def kv_home(which, at_core, n):
        return kv.at[n, which, at_core, xpos]

    def home_copies(n, head):
        at = rows_of(n)
        k = (n * 2 + head) * 2
        r = (n * 2 + yhi) * 2
        target = {"ctx": block_of(head, xpos, ylo), "mp": core * PLANE + zpos}
        return (
            remote(
                kv_out.at[head, at, :], kv_home(yhi, ylo, n),
                h_send.at[k], h_recv.at[r], **target,
            ),
            remote(
                q_out.at[head, at, :], qs.at[yhi, at, :],
                h_send.at[k + 1], h_recv.at[r + 1], **target,
            ),
        )

    def local_copies(n, head):
        at = rows_of(n)
        return (
            pltpu.make_async_copy(
                kv_out.at[head, at, :], kv_home(yhi, ylo, n), l_sem.at[n * 2]
            ),
            pltpu.make_async_copy(
                q_out.at[head, at, :], qs.at[yhi, at, :], l_sem.at[n * 2 + 1]
            ),
        )

    def home_waits(n, which):
        at = rows_of(n)
        k = (n * 2 + which) * 2
        at_home = jnp.logical_and(same, yhi == which)

        @pl.when(at_home)
        def _():
            for copy in local_copies(n, which):
                copy.wait()

        @pl.when(jnp.logical_not(at_home))
        def _():
            target = {"ctx": block_of(which, xpos, ylo), "mp": core * PLANE + zpos}
            remote(
                kv_out.at[0, at, :], kv_home(which, core, n),
                h_send.at[k], h_recv.at[k], **target,
            ).wait_recv()
            remote(
                q_out.at[0, at, :], qs.at[which, at, :], h_send.at[k + 1], h_recv.at[k + 1],
                **target,
            ).wait_recv()

    def ring_copy(n, step, direction, outgoing):
        sign = 3 if direction == 0 else 1
        away = step - 1 if outgoing else step
        at = slice(0, part) if step == 1 else slice(direction * half, direction * half + half)
        ref = kv.at[n, :, core, (xpos + sign * away) % 4, at, :]
        k = (n * 2 + step - 1) * 2 + direction
        return remote(
            ref, ref, r_send.at[k], r_recv.at[k], ctx=x_right if direction == 0 else x_left
        )

    def core_copy(n, outgoing):
        ref = kv.at[n, :, core if outgoing else 1 - core]
        return remote(ref, ref, c_send.at[n], c_recv.at[n], ctx=sibling)

    def ring_begin(n):
        for which in (0, 1):
            home_waits(n, which)
        for direction in (0, 1):
            ring_copy(n, 1, direction, True).start()

    def ring_tick(n, step):
        for direction in (0, 1):
            ring_copy(n, step, direction, False).wait_recv()
            if step == 1:
                ring_copy(n, 2, direction, True).start()
        if step == 2:
            core_copy(n, True).start()

    def ring_end(n):
        core_copy(n, False).wait_recv()

    def project(n):
        d_copy(n, False).wait_recv()
        at = rows_of(n)
        wide = x[at, :].astype(jnp.float32)
        squares = jnp.sum(wide * wide, axis=1, keepdims=True)
        norm = lax.rsqrt(squares / all_chans + NORM_EPSILON)
        for j in range(3):
            scale = norm * (math.log2(math.e) / math.sqrt(HEAD_DIM)) if j == 0 else norm
            made = jnp.dot(x[at, :], w[j], preferred_element_type=jnp.float32) * scale
            made = made.astype(jnp.bfloat16)
            for head in (0, 1):
                piece = made[:, head * HEAD_DIM : (head + 1) * HEAD_DIM]
                if j == 0:
                    q_out[head, at, :] = piece
                else:
                    kv_out[head, at, (j - 1) * HEAD_DIM : j * HEAD_DIM] = piece
        for head in (0, 1):
            stays = jnp.logical_and(same, yhi == head)

            @pl.when(stays)
            def _(head=head):
                for copy in local_copies(n, head):
                    copy.start()

            @pl.when(jnp.logical_not(stays))
            def _(head=head):
                for copy in home_copies(n, head):
                    copy.start()

    ones = jnp.ones((span // 2, HEAD_DIM), jnp.bfloat16)

    def scores_of(queries, block):
        return lax.dot_general(
            queries, block[:, :HEAD_DIM], (((1,), (1,)), ((), ())),
            preferred_element_type=jnp.float32,
        )

    def masked(scores, bounds):
        width = scores.shape[1] // 2
        col = lax.broadcasted_iota(jnp.int32, (part, width), 1)
        return jnp.concatenate(
            [
                jnp.where(col < bound, scores[:, i * width : (i + 1) * width], NEG_FILL)
                for i, bound in enumerate(bounds)
            ],
            axis=1,
        )

    def pair(q_chunk, k_chunk):
        at = rows_of(q_chunk)
        row = lax.broadcasted_iota(jnp.int32, (part, 1), 0) + 1
        extra = jnp.where(k_chunk < q_chunk, part, jnp.where(k_chunk == q_chunk, row, 0))
        bounds = [
            xpos * part + jnp.where(core == 0, extra, part),
            xpos * part + jnp.where(core == 0, 0, extra),
        ]
        low = kv[k_chunk, 0].reshape(span // 2, 2 * HEAD_DIM)
        high = kv[k_chunk, 1].reshape(span // 2, 2 * HEAD_DIM)
        for which in (1, 0):
            queries = qs[which, at, :]
            if which == 1:
                blocks = [low, high]
                scores = [scores_of(queries, low), masked(scores_of(queries, high), bounds)]
            else:
                blocks = [low]
                scores = [masked(scores_of(queries, low), bounds)]
            old = q_max[which, at, :]
            new = old
            for s in scores:
                new = jnp.maximum(new, jnp.max(s, axis=1, keepdims=True))
            wide = jnp.concatenate([new] * (span // 256), axis=1)
            shrink = jnp.exp2(old - new)
            total = q_acc[which, at, :] * jnp.concatenate([shrink, shrink], axis=1)
            for s, block in zip(scores, blocks):
                weights = jnp.exp2(s - wide).astype(jnp.bfloat16)
                values = jnp.concatenate([block[:, HEAD_DIM:], ones], axis=1)
                total = total + jnp.dot(weights, values, preferred_element_type=jnp.float32)
            q_acc[which, at, :] = total
            q_max[which, at, :] = new

    def early_pairs(n, first, last):
        def one(i, carry):
            pair(n, i)
            return carry

        lax.fori_loop(first, last, one, 0)

    def late_pairs(n, first, last):
        def one(i, carry):
            pair(i, n)
            return carry

        lax.fori_loop(first, last, one, 0)

    head_lanes = pl.ds(pl.multiple_of(yhi * HEAD_DIM, HEAD_DIM), HEAD_DIM)
    other_lanes = pl.ds(pl.multiple_of((1 - yhi) * HEAD_DIM, HEAD_DIM), HEAD_DIM)

    def o_copy(m, lanes):
        at = rows_of(m)
        return remote(
            o_out.at[1 - yhi, at, :], att.at[at, lanes], o_send.at[m], o_recv.at[m], ctx=opposite
        )

    def finish(m):
        at = rows_of(m)
        for which in (0, 1):
            done = q_acc[which, at, :HEAD_DIM] / q_acc[which, at, HEAD_DIM:]
            o_out[which, at, :] = done.astype(jnp.bfloat16)
        o_copy(m, head_lanes).start()
        att[at, head_lanes] = o_out[yhi, at, :]

    def round_of(it, carry):
        def when(n):
            return pl.when(jnp.logical_and(n >= 0, n < CHUNKS))

        def some_early(n, piece):
            @when(n)
            def _():
                early_pairs(n, n * piece // 2, n * (piece + 1) // 2)

        def some_late(n, piece):
            @pl.when(jnp.logical_and(n >= 0, n < CHUNKS - 1))
            def _():
                count = n + 1
                late_pairs(n, count * piece // 3, count * (piece + 1) // 3)

        def w_at(at_round, *ticks):
            @pl.when(it == at_round)
            def _():
                w_ticks(*ticks)

        @when(it)
        def _():
            begin(it)

        w_at(0, (0, 4), (0, 5), (1, 1))
        w_at(1, (1, 2))

        @when(it - 2)
        def _():
            arrive(it - 2, 2)

        w_at(2, (2, 1), (1, 4))
        w_at(3, (2, 4))

        @when(it - 1)
        def _():
            arrive(it - 1, 1)

        w_at(1, (2, 0), (1, 3))
        w_at(2, (2, 2))
        some_late(it - 7, 2)

        @when(it - 6)
        def _():
            ring_end(it - 6)

        some_late(it - 6, 0)

        @when(it - 5)
        def _():
            ring_tick(it - 5, 1)

        @when(it - 3)
        def _():
            arrive(it - 3, 4)

        some_late(it - 6, 1)

        @when(it - 4)
        def _():
            ring_begin(it - 4)

        some_early(it - 4, 0)

        @pl.when(it == 3)
        def _():
            w_ticks((2, 5))

            @pl.when(same)
            def _():
                w_copy.wait()

        @when(it - 3)
        def _():
            project(it - 3)

        some_early(it - 5, 1)

        @when(it - 5)
        def _():
            ring_tick(it - 5, 2)

        @when(it - 2)
        def _():
            arrive(it - 2, 3)

        w_at(2, (1, 5), (2, 3))
        return carry

    lax.fori_loop(0, CHUNKS + 6, round_of, 0)

    last = CHUNKS - 1

    def closing(m, carry):
        pair(m, last)
        finish(m)
        return carry

    lax.fori_loop(0, CHUNKS, closing, 0)

    for m in range(CHUNKS):
        o_copy(m, other_lanes).wait_recv()
    att_copy = pltpu.make_async_copy(att, att_hbm, local_sem.at[3])
    att_copy.start()

    rim_copy.wait_send()
    for k in range(1, CTX):

        @pl.when(me + k < CTX)
        def _(k=k):
            state_copy(k, me).wait_send()

    @pl.when(crossed)
    def _():
        for i in range(6):
            wy_copy(i).wait_send()
            for step in (1, 2):
                for direction in (0, 1):
                    wx_copy(i, step, direction, True).wait_send()

    def sent(n, carry):
        @pl.when(crossed)
        def _():
            y_copy(n).wait_send()

        for direction in (0, 1):
            for step in (1, 2, 3, 4):
                z_copy(n, step, direction, True).wait_send()
            for step in (1, 2):
                ring_copy(n, step, direction, True).wait_send()
        d_copy(n, True).wait_send()
        core_copy(n, True).wait_send()
        for which in (0, 1):

            @pl.when(jnp.logical_not(jnp.logical_and(same, yhi == which)))
            def _(which=which):
                for copy in home_copies(n, which):
                    copy.wait_send()

        o_copy(n, head_lanes).wait_send()
        return carry

    lax.fori_loop(0, CHUNKS, sent, 0)
    hyena_copy.wait()
    att_copy.wait()


def hand_over(a_ref, b_ref, a_out, b_out):
    a_out[...] = a_ref[...]
    b_out[...] = b_ref[...]


def per_device(token_ids, feature_table, short_filter, rates, residues, skip_weight, w_qkv):
    rows = token_ids.shape[0]
    vocab, _, chans = feature_table.shape
    modes = rates.shape[1]
    all_chans, _, width = w_qkv.shape
    f32, bf16 = jnp.float32, jnp.bfloat16
    dma = pltpu.SemaphoreType.DMA
    vmem = pl.BlockSpec(memory_space=pltpu.VMEM)
    hbm = pl.BlockSpec(memory_space=pl.ANY)
    made = pl.pallas_call(
        mixer_kernel,
        out_shape=(
            jax.ShapeDtypeStruct((rows, chans), bf16),
            jax.ShapeDtypeStruct((rows, width), bf16),
        ),
        in_specs=[vmem, hbm, vmem, vmem, vmem, vmem, hbm],
        out_specs=(hbm, hbm),
        scratch_shapes=[
            pltpu.VMEM((3, vocab, chans), bf16),
            pltpu.VMEM((rows, vocab), bf16),
            pltpu.VMEM((3, all_chans, width), bf16),
            pltpu.VMEM((3, 8 + rows, chans), f32),
            pltpu.VMEM((chans // 128, rows, 128), f32),
            pltpu.VMEM((chans // 128, rows, 128), f32),
            pltpu.VMEM((chans // 128, rows, 128), f32),
            pltpu.VMEM((rows // 128, 128), jnp.int32),
            pltpu.VMEM((modes, SEGS, chans), f32),
            pltpu.VMEM((modes, SEGS, chans), f32),
            pltpu.VMEM((modes, SEGS, chans), f32),
            pltpu.VMEM((modes, SEGS, chans), f32),
            pltpu.VMEM((CTX, modes, chans), f32),
            pltpu.VMEM((rows, chans), bf16),
            pltpu.VMEM((rows, all_chans), bf16),
            pltpu.VMEM((CHUNKS, 2, 2, 4, rows // CHUNKS, 2 * HEAD_DIM), bf16),
            pltpu.VMEM((2, rows, HEAD_DIM), bf16),
            pltpu.VMEM((2, rows, 2 * HEAD_DIM), bf16),
            pltpu.VMEM((2, rows, HEAD_DIM), bf16),
            pltpu.VMEM((2, rows, 2 * HEAD_DIM), f32),
            pltpu.VMEM((2, rows, HEAD_DIM), f32),
            pltpu.VMEM((2, rows, HEAD_DIM), bf16),
            pltpu.VMEM((rows, width), bf16),
            dma((4,)),
            dma((2,)),
            dma((CTX - 1,)),
            dma((CTX - 1,)),
            dma((6,)),
            dma((6,)),
            dma((24,)),
            dma((24,)),
            dma((CHUNKS,)),
            dma((CHUNKS,)),
            dma((CHUNKS * 8,)),
            dma((CHUNKS * 8,)),
            dma((CHUNKS,)),
            dma((CHUNKS,)),
            dma((CHUNKS * 4,)),
            dma((CHUNKS * 4,)),
            dma((CHUNKS * 2,)),
            dma((CHUNKS,)),
            dma((CHUNKS,)),
            dma((CHUNKS * 4,)),
            dma((CHUNKS * 4,)),
            dma((CHUNKS,)),
            dma((CHUNKS,)),
        ],
        compiler_params=pltpu.CompilerParams(
            collective_id=0, has_side_effects=True, vmem_limit_bytes=56 * 1024 * 1024
        ),
        name="mixer",
    )(
        token_ids.reshape(rows // 128, 128),
        jnp.transpose(feature_table, (1, 0, 2)),
        short_filter,
        rates.T,
        residues.T,
        skip_weight.reshape(1, chans),
        jnp.transpose(w_qkv, (1, 0, 2)),
    )
    return pl.pallas_call(
        hand_over,
        out_shape=tuple(jax.ShapeDtypeStruct(a.shape, a.dtype) for a in made),
        grid=(2,),
        in_specs=[pl.BlockSpec((rows // 2, a.shape[1]), lambda i: (i, 0)) for a in made],
        out_specs=tuple(pl.BlockSpec((rows // 2, a.shape[1]), lambda i: (i, 0)) for a in made),
        name="hand_over",
    )(*made)


def solution(mesh):
    in_specs = (
        P("ctx"),
        P(None, None, "mp"),
        P(None, None, "mp"),
        P("mp", None),
        P("mp", None),
        P("mp"),
        P(None, None, "mp"),
    )
    out_specs = (P("ctx", "mp"), P("ctx", "mp"))
    return jax.shard_map(
        per_device, mesh=mesh, in_specs=in_specs, out_specs=out_specs, check_vma=False
    )
```
